32 devices in a mesh: view: 16 (over z, y, x), head: 2 (over core).
Axes of the slice: x: 2, y: 2, z: 4, core: 2. Of those that a mesh axis runs over, the one named last changes fastest.
Arguments:
- tokens: bfloat16 [2, 16, 128, 1024], P(None, 'view'), may hold values from -6 to 6
- queries: bfloat16 [2, 16, 128, 1024], P(None, 'view', None, 'head'), may hold values from -8 to 8
- keys: bfloat16 [2, 16, 128, 1024], P(None, 'view', None, 'head'), may hold values from -8 to 8
- values: bfloat16 [2, 16, 128, 1024], P(None, 'view', None, 'head'), may hold values from -6 to 6
- w_qkv: bfloat16 [3, 1024, 1024], P(None, None, 'head'), may hold values from -0.1875 to 0.1875
- w_out: bfloat16 [1024, 1024], P('head'), may hold values from -0.1875 to 0.1875
- d_out: bfloat16 [2, 16, 128, 1024], P(None, 'view'), may hold values from -6 to 6
- neighbours: int32 [16, 8], replicated, may hold values from 0 to 15, as said below
- degrees: int32 [16], replicated, may hold values from 4 to 8, as said below
Outputs:
- d_tokens: bfloat16 [2, 16, 128, 1024], P(None, 'view', None, 'head')
- d_wqkv: float32 [3, 1024, 1024], P(None, 'view', 'head')
- d_wo: float32 [1024, 1024], P('head', 'view')
The draws below stay inside these ranges and needn't reach their ends.
Inputs may be any that keep to these rules, and one draw needn't show every extreme that they name: Row c lists cameras c + o modulo 16 for the 8 offsets o with 0 < |o| <= 4, each once, in an order drawn per camera; its first degrees[c] entries are c's neighbours. `degrees`: some camera has 8 neighbours and some has 4.
All inputs are finite; a program needn't handle non-finite values.
Results may differ from the reference program's by a relative error of at most 0.018.
Values may be sent and summed in bfloat16 or wider, within the bound.
No kernel may reach another device: no remote copies, remote signals or barrier semaphores. Data moves between devices by JAX's collectives and lax.ppermute only.
A program may use at most 128 MiB of HBM per device.

```python
import jax
import jax.numpy as jnp
from jax import lax

D = 1024
H = 16
HD = 64
SCENES = 2
REACH = 4
MAXDEG = 8
TOK = 128
CAMS = 16


def camera_graph(key):
    key_order = jax.random.fold_in(key, 21)
    key_count = jax.random.fold_in(key, 22)
    key_pick = jax.random.fold_in(key, 23)
    ranking = jax.random.randint(key_order, (CAMS, MAXDEG), 0, 2 ** 20) * MAXDEG + jnp.arange(MAXDEG, dtype=jnp.int32)[None, :]
    order = jnp.argsort(ranking, axis=1).astype(jnp.int32)
    offset = jnp.where(order < REACH, order - REACH, order - REACH + 1)
    neighbours = ((jnp.arange(CAMS, dtype=jnp.int32)[:, None] + offset) % CAMS).astype(jnp.int32)
    counts = jax.random.randint(key_count, (CAMS,), MAXDEG // 2, MAXDEG + 1)
    picks = jax.random.randint(key_pick, (2,), 0, CAMS)
    first = picks[0]
    second = (first + 1 + picks[1] % (CAMS - 1)) % CAMS
    counts = counts.at[first].set(MAXDEG).at[second].set(MAXDEG // 2)
    return (neighbours, counts.astype(jnp.int32))


def draw_queries(key, part):
    key = jax.random.fold_in(key, 7)
    shape = (SCENES, CAMS, TOK, H * HD)
    base = jnp.clip(jax.random.normal(key, shape, jnp.float32), -6.0, 6.0)
    return base.astype(jnp.bfloat16)


def draw_keys(key, part):
    key = jax.random.fold_in(key, 13)
    shape = (SCENES, CAMS, TOK, H * HD)
    base = jnp.clip(jax.random.normal(key, shape, jnp.float32), -6.0, 6.0)
    return base.astype(jnp.bfloat16)


def draw_neighbours(key, part):
    return camera_graph(key)[0]


def draw_degrees(key, part):
    return camera_graph(key)[1]


def strengthened(result, key, source, target, parts, factor):
    owner, partner = [(jnp.arange(result.shape[dim]) // (result.shape[dim] // parts)).reshape([-1 if axis == dim else 1 for axis in range(result.ndim)]) for dim in (source, target)]
    chosen = jax.random.permutation(key, parts)[partner]
    strong = (owner == chosen) | (owner == (partner + parts // 2) % parts)
    return jnp.where(strong, factor * result, result)


def block_scale(own_key, extent, split, low, high):
    def one(dim, shards_of):
        heights = jax.random.uniform(jax.random.fold_in(jax.random.fold_in(own_key, 6), dim), (shards_of,), jnp.float32, low / len(split), high / len(split))
        return jnp.repeat(jnp.exp(heights), extent[dim] // shards_of).reshape((-1,) + (1,) * (len(extent) - dim - 1))

    factor_of = one(*split[0])
    for cut in split[1:]:
        factor_of = factor_of * one(*cut)
    return factor_of


def gaussian(rng, extent, width, bound, shards=(), held_as=jnp.bfloat16):
    values = width * jax.random.normal(rng, extent, jnp.float32)
    if shards:
        values = values * block_scale(rng, extent, shards, -0.22, 0.18)
    return jnp.clip(values, -bound, bound).astype(held_as)


def heavy_noise(own_key, shape, spread, limit, shards, heavy, kind=jnp.bfloat16):
    values = spread * jax.random.normal(own_key, shape, jnp.float32)
    if shards:
        values = values * block_scale(own_key, shape, shards, -0.22, 0.18)
    return jnp.clip(strengthened(values, jax.random.fold_in(own_key, 3), *heavy), -limit, limit).astype(kind)


def setup_inputs(seed: int = 0) -> dict:
    splits = jax.random.split(jax.random.key(seed), 10)
    tokens = heavy_noise(splits[0], (SCENES, CAMS, TOK, D), 1.0, 6.0, ((1, 16),), (1, 3, 16, 2.0))
    queries = draw_queries(jax.random.fold_in(splits[9], 71), 0)
    keys = draw_keys(jax.random.fold_in(splits[9], 71), 0)
    values = gaussian(splits[3], (SCENES, CAMS, TOK, H * HD), 1.0, 6.0, ((1, 16), (3, 2)))
    w_qkv = gaussian(splits[4], (3, D, H * HD), D ** -0.5, 0.1875, ((2, 2),))
    w_out = gaussian(splits[5], (H * HD, D), (H * HD) ** -0.5, 0.1875, ((0, 2),))
    d_out = heavy_noise(splits[6], (SCENES, CAMS, TOK, D), 1.0, 6.0, ((1, 16),), (1, 3, 16, 2.0))
    neighbours = draw_neighbours(jax.random.fold_in(splits[9], 71), 0)
    degrees = draw_degrees(jax.random.fold_in(splits[9], 71), 0)
    return {"tokens": tokens, "queries": queries, "keys": keys, "values": values, "w_qkv": w_qkv, "w_out": w_out, "d_out": d_out, "neighbours": neighbours, "degrees": degrees}


def offsets_list():
    return [step for step in range(-REACH, REACH + 1) if step != 0]


def edge_table(neighbours, degrees):
    cameras = jnp.arange(CAMS, dtype=jnp.int32)
    slots = jnp.arange(MAXDEG, dtype=jnp.int32)
    live = slots[None, :] < degrees[:, None]
    rows = []
    for offset in offsets_list():
        target = (cameras + offset) % CAMS
        hit = jnp.logical_and(neighbours == target[:, None], live)
        rows.append(jnp.where(jnp.any(hit, axis=1), 1.0, 0.0).astype(jnp.float32))
    return rows


def rounded(value):
    return lax.optimization_barrier(value.astype(jnp.bfloat16)).astype(jnp.float32)


def head_grads(pack, masks):
    query, key_arr, value_arr, d_head = [part.astype(jnp.float32) for part in pack]
    scale = HD ** -0.5
    shifts = [0] + offsets_list()
    weights = [jnp.ones((CAMS,), jnp.float32)] + masks

    def moved(arr, offset):
        return jnp.roll(arr, -offset, axis=1)

    def scores(offset):
        return jnp.einsum('sctd,scud->sctu', query, moved(key_arr, offset)) * scale

    top = None
    for offset, weight in zip(shifts, weights):
        peak = jnp.where(weight[None, :, None] > 0, jnp.max(scores(offset), axis=3), -jnp.inf)
        top = peak if top is None else jnp.maximum(top, peak)
    total = jnp.zeros(top.shape, jnp.float32)
    for offset, weight in zip(shifts, weights):
        prob = jnp.exp(scores(offset) - top[..., None]) * weight[None, :, None, None]
        total = total + jnp.sum(prob, axis=3)
    lse = top + jnp.log(total)
    accum = jnp.zeros(query.shape, jnp.float32)
    for offset, weight in zip(shifts, weights):
        prob_low = rounded(jnp.exp(scores(offset) - lse[..., None]) * weight[None, :, None, None])
        accum = accum + jnp.einsum('sctu,scud->sctd', prob_low, moved(value_arr, offset))
    attended = rounded(accum)
    delta = jnp.sum(d_head * attended, axis=3)
    d_query = jnp.zeros(query.shape, jnp.float32)
    d_key = jnp.zeros(query.shape, jnp.float32)
    d_value = jnp.zeros(query.shape, jnp.float32)
    for offset, weight in zip(shifts, weights):
        keys_here = moved(key_arr, offset)
        values_here = moved(value_arr, offset)
        prob = jnp.exp(scores(offset) - lse[..., None]) * weight[None, :, None, None]
        prob_low = rounded(prob)
        d_value = d_value + jnp.roll(jnp.einsum('sctu,sctd->scud', prob_low, d_head), offset, axis=1)
        d_prob = jnp.einsum('sctd,scud->sctu', d_head, values_here)
        d_score = rounded(prob * (d_prob - delta[..., None]))
        d_query = d_query + jnp.einsum('sctu,scud->sctd', d_score, keys_here) * scale
        d_key = d_key + jnp.roll(jnp.einsum('sctu,sctd->scud', d_score, query) * scale, offset, axis=1)
    return attended, d_query, d_key, d_value


def reference(tokens, queries, keys, values, w_qkv, w_out, d_out, neighbours, degrees):
    masks = edge_table(neighbours, degrees)
    d_head = jnp.einsum('sctd,ed->scte', d_out.astype(jnp.float32), w_out.astype(jnp.float32)).astype(jnp.bfloat16)

    def per_head(arr):
        return jnp.moveaxis(arr.reshape(SCENES, CAMS, TOK, H, HD), 3, 0)

    def merged(arr):
        return jnp.moveaxis(arr, 0, 3).reshape(SCENES, CAMS, TOK, H * HD)

    packs = (per_head(queries), per_head(keys), per_head(values), per_head(d_head))
    attended, d_query, d_key, d_value = lax.map(lambda pack: head_grads(pack, masks), packs)
    attended = merged(attended)
    grads = jnp.stack([merged(d_query), merged(d_key), merged(d_value)]).astype(jnp.bfloat16).astype(jnp.float32)
    d_tokens = jnp.einsum('jscte,jde->sctd', grads, w_qkv.astype(jnp.float32)).astype(jnp.bfloat16)
    d_wqkv = jnp.einsum('sctd,jscte->jde', tokens.astype(jnp.float32), grads)
    d_wo = jnp.einsum('scte,sctd->ed', attended, d_out.astype(jnp.float32))
    return d_tokens, d_wqkv, d_wo
```

```python
import functools

import jax
import jax.numpy as jnp
from jax import lax
from jax.experimental import pallas as pl
from jax.experimental.pallas import tpu as pltpu
from jax.sharding import PartitionSpec as P

HD = 64
LANE = 128
QUAD = 4
BF = jnp.bfloat16
F32 = jnp.float32
MIB = 2**20
OFF = -1e30


def params(mib):
    return pltpu.CompilerParams(vmem_limit_bytes=mib * MIB)


def vmem(count):
    return [pl.BlockSpec(memory_space=pltpu.VMEM)] * count


def cost(flops, moved):
    return pl.CostEstimate(flops=flops, bytes_accessed=moved, transcendentals=0)


def mul(a, b):
    return jnp.dot(a, b, preferred_element_type=F32)


def mul_nt(a, b):
    return lax.dot_general(a, b, (((1,), (1,)), ((), ())), preferred_element_type=F32)


def slot_of(view):
    plane, quad = view // QUAD, view % QUAD
    return quad // 2, 2 * plane + quad % 2


def pack_qk_kernel(q_ref, k_ref, out_ref):
    scenes = q_ref.shape[0]
    turned = []
    for scene in range(scenes):
        turned.append((q_ref[scene, 0].T * HD**-0.5, k_ref[scene, 0].T))
    for view in range(out_ref.shape[0]):
        scene, head = slot_of(view)
        qry, key = turned[scene]
        out_ref[view, :HD] = qry[head * HD : (head + 1) * HD].astype(BF)
        out_ref[view, HD:] = key[head * HD : (head + 1) * HD]


def pack_vd_kernel(v_ref, d_ref, w_ref, out_ref):
    scenes = v_ref.shape[0]
    turned = []
    for scene in range(scenes):
        d_head = mul_nt(w_ref[...], d_ref[scene, 0]).astype(BF)
        turned.append((v_ref[scene, 0].T, d_head))
    for view in range(out_ref.shape[0]):
        scene, head = slot_of(view)
        val, d_head = turned[scene]
        out_ref[view, :HD] = val[head * HD : (head + 1) * HD]
        out_ref[view, HD:] = d_head[head * HD : (head + 1) * HD]


def attend_kernel(reach, pos_ref, bias_ref, qk_ref, vd_ref, *rest):
    outs, (k_row, v_row, k_col, v_col, dk_acc, dv_acc, s_buf, p_buf, d_buf, att_buf, dq_buf) = rest[:QUAD], rest[QUAD:]
    cameras = qk_ref.shape[0]
    span = 2 * reach + 2
    two = 2 * LANE
    for place in range(cameras + 2 * reach):
        cam = (place - reach) % cameras
        rows = pl.ds(place * LANE, LANE)
        key, val = qk_ref[cam, HD:], vd_ref[cam, :HD]
        k_col[:, rows] = key
        v_col[:, rows] = val
        k_row[rows, :] = key.T
        v_row[rows, :] = val.T
    dk_acc[...] = jnp.zeros_like(dk_acc)
    dv_acc[...] = jnp.zeros_like(dv_acc)

    def step(i, carry):
        base = pl.multiple_of(i * two, two)
        q_col = jnp.concatenate([qk_ref[2 * i, :HD], qk_ref[2 * i + 1, :HD]], axis=1)
        d_col = jnp.concatenate([vd_ref[2 * i, HD:], vd_ref[2 * i + 1, HD:]], axis=1)
        q_rows, d_rows = q_col.T, d_col.T
        bias = bias_ref[i]

        def at(j):
            return pl.ds(pl.multiple_of(base + j * LANE, LANE), LANE)

        top = None
        for j in range(span):
            score = mul(k_row[at(j), :], q_col)
            s_buf[j] = score
            peak = jnp.max(score, axis=0, keepdims=True) + bias[j : j + 1]
            top = peak if top is None else jnp.maximum(top, peak)
        total = jnp.zeros((8, two), F32)
        for j in range(span):
            prob = jnp.exp(s_buf[j] + (bias[j : j + 1] - top))
            s_buf[j] = prob
            total = total + jnp.sum(prob.reshape(LANE // 8, 8, two), axis=0)
        inv = 1.0 / jnp.sum(total, axis=0, keepdims=True)
        for j in range(span):
            prob = s_buf[j] * inv
            s_buf[j] = prob
            low = prob.astype(BF)
            p_buf[j * LANE : (j + 1) * LANE] = low
            dv_acc[at(j), :] += mul(low, d_rows)
        window = pl.ds(base, span * LANE)
        att = mul(v_col[:, window], p_buf[...]).astype(BF)
        delta = jnp.sum(att.astype(F32) * d_col.astype(F32), axis=0, keepdims=True)
        for j in range(span):
            d_score = (s_buf[j] * (mul(v_row[at(j), :], d_col) - delta)).astype(BF)
            d_buf[j * LANE : (j + 1) * LANE] = d_score
            dk_acc[at(j), :] += mul(d_score, q_rows)
        dq = (mul(k_col[:, window], d_buf[...]) * HD**-0.5).astype(BF)
        for t in range(2):
            att_buf[2 * i + t] = att[:, t * LANE : (t + 1) * LANE]
            dq_buf[2 * i + t] = dq[:, t * LANE : (t + 1) * LANE]
        return carry

    lax.fori_loop(0, cameras // 2, step, 0)
    for acc in (dk_acc, dv_acc):
        acc[cameras * LANE : (cameras + reach) * LANE] += acc[: reach * LANE]
        acc[reach * LANE : 2 * reach * LANE] += acc[(cameras + reach) * LANE :]
    quad = pos_ref[1]
    for k in range(QUAD):
        for plane in range(cameras // QUAD):
            cam = plane * QUAD + (quad ^ k)
            rows = pl.ds(pl.multiple_of((cam + reach) * LANE, LANE), LANE)
            outs[k][plane, :HD] = att_buf[cam]
            outs[k][plane, HD : 2 * HD] = dq_buf[cam]
            outs[k][plane, 2 * HD : 3 * HD] = dk_acc[rows, :].T.astype(BF)
            outs[k][plane, 3 * HD :] = dv_acc[rows, :].T.astype(BF)


def weights_kernel(planes, pos_ref, *refs):
    blocks, own, other = refs[:QUAD], refs[QUAD : QUAD + planes], refs[QUAD + planes : QUAD + 2 * planes]
    outs = refs[QUAD + 2 * planes : 2 * QUAD + 2 * planes]
    buf, left, left_o, tok, d_o, wide = refs[2 * QUAD + 2 * planes :]
    plane, quad, core = pos_ref[0], pos_ref[1], pos_ref[2]
    for k in range(QUAD):
        buf[quad ^ k] = blocks[k][...]
    for k in range(planes):
        cam = lax.rem(plane - k + planes, planes)
        for order, (ref, scene) in enumerate(((own[k], core), (other[k], 1 - core))):
            at = (2 * k + order) * LANE
            tok[at : at + LANE] = ref[:LANE]
            d_o[at : at + LANE] = ref[LANE:]
            for half in range(2):
                block = buf[2 * scene + half, cam]
                left_o[half * HD : (half + 1) * HD, at : at + LANE] = block[:HD]
                for j in range(3):
                    row = (2 * j + half) * HD
                    left[row : row + HD, at : at + LANE] = block[(j + 1) * HD : (j + 2) * HD]
    wide[:, : 6 * HD] = mul(left[...], tok[...]).T
    wide[:, 6 * HD :] = mul(left_o[...], d_o[...]).T
    part = wide.shape[0] // (QUAD * planes)
    for k in range(QUAD):
        for p in range(planes):
            rows = pl.ds(pl.multiple_of((p * QUAD + (quad ^ k)) * part, part), part)
            outs[k][p * part : (p + 1) * part] = wide[rows, :].astype(BF)


def sum_kernel(planes, pos_ref, *refs):
    terms, outs, total = refs[:QUAD], refs[QUAD : QUAD + planes], refs[QUAD + planes]
    plane = pos_ref[0]
    acc = terms[0][...].astype(F32)
    for term in terms[1:]:
        acc = acc + term[...].astype(F32)
    total[...] = acc
    part = total.shape[0] // planes
    for k in range(planes):
        rows = pl.ds(pl.multiple_of((plane ^ k) * part, part), part)
        outs[k][...] = total[rows, :].astype(BF)


def finish_kernel(planes, pos_ref, *refs):
    terms, (w_ref, o_ref), buf = refs[:planes], refs[planes : planes + 2], refs[planes + 2]
    plane = pos_ref[0]
    for k in range(planes):
        buf[plane ^ k] = terms[k][...].astype(F32)
    two = 2 * HD
    for p in range(planes):
        for j in range(3):
            w_ref[j, :, p * two : (p + 1) * two] = buf[p, :, j * two : (j + 1) * two]
        o_ref[p * two : (p + 1) * two, :] = buf[p, :, 3 * two :].T


def inputs_kernel(planes, pos_ref, *refs):
    blocks, w_ref, (mine, theirs), (buf, turned) = refs[:planes], refs[planes], refs[planes + 1 : planes + 3], refs[planes + 3 :]
    plane, core = pos_ref[0], pos_ref[2]
    for k in range(planes):
        buf[plane ^ k] = blocks[k][...]
    width = w_ref.shape[2]
    for scene in range(2):
        for j in range(3):
            for p in range(planes):
                for half in range(2):
                    row = (2 * p + half) * HD
                    turned[scene, j, row : row + HD] = buf[p, 2 * scene + half, j * HD : (j + 1) * HD]
    left = [
        jnp.concatenate([turned[scene, j].T for scene in range(2)], axis=0) for j in range(3)
    ]
    half = w_ref.shape[1] // 2
    for ref, who in ((theirs, 1 - core), (mine, core)):
        rows = pl.ds(pl.multiple_of(who * half, half), half)
        acc = mul_nt(left[0], w_ref[0, rows, :])
        for j in range(1, 3):
            acc = acc + mul_nt(left[j], w_ref[j, rows, :])
        ref[...] = acc


def split_body(tokens, queries, keys, values, w_qkv, w_out, d_out, neighbours, degrees):
    cameras = neighbours.shape[0]
    reach = neighbours.shape[1] // 2
    planes = cameras // QUAD
    scenes, _, rows, width = queries.shape
    model = tokens.shape[3]
    view, core = lax.axis_index("view"), lax.axis_index("head")
    plane, quad = view // QUAD, view % QUAD
    pos = jnp.stack([plane, quad, core]).astype(jnp.int32)
    smem = [pl.BlockSpec(memory_space=pltpu.SMEM)]

    def shape(*dims, dtype=BF):
        return jax.ShapeDtypeStruct(dims, dtype)

    def along(value, pairs):
        return lax.ppermute(value, "view", pairs)

    every = range(cameras)

    def quad_swap(value, k):
        return along(value, [(i, i ^ k) for i in every])

    def plane_swap(value, k):
        return along(value, [(i, i ^ (k * QUAD)) for i in every])

    def other_core(value):
        return lax.ppermute(value, "head", [(0, 1), (1, 0)])

    qk = pl.pallas_call(
        pack_qk_kernel,
        out_shape=shape(cameras, 2 * HD, rows),
        in_specs=vmem(2),
        out_specs=vmem(1)[0],
        compiler_params=params(16),
        name="pack_qk",
    )(queries, keys)
    qk = lax.all_to_all(qk, "view", 0, 0, tiled=True)
    vd = pl.pallas_call(
        pack_vd_kernel,
        out_shape=shape(cameras, 2 * HD, rows),
        in_specs=vmem(3),
        out_specs=vmem(1)[0],
        compiler_params=params(16),
        name="pack_vd",
    )(values, d_out, w_out)
    vd = lax.all_to_all(vd, "view", 0, 0, tiled=True)

    pair = jnp.concatenate(
        [lax.dynamic_index_in_dim(arr, core, 0, keepdims=False)[0] for arr in (tokens, d_out)], axis=0
    )
    own = [pair]
    for k in range(1, planes):
        own.append(along(own[-1], [(i, (i + QUAD) % cameras) for i in every]))
    other = [other_core(value) for value in own]

    span = 2 * reach + 2
    offset = jnp.arange(span)[None, :, None] - reach - jnp.arange(2)[None, None, :]
    query = (2 * jnp.arange(cameras // 2))[:, None, None] + jnp.arange(2)[None, None, :]
    target = (query + offset) % cameras
    listed = neighbours.reshape(cameras // 2, 1, 2, 2 * reach)
    count = degrees.reshape(cameras // 2, 1, 2, 1)
    live = jnp.arange(2 * reach)[None, None, None, :] < count
    hit = jnp.any((listed == target[..., None]) & live, axis=3) & (jnp.abs(offset) <= reach)
    bias = jnp.where(hit | (offset == 0), 0.0, OFF).astype(F32)
    bias = jnp.repeat(bias, rows, axis=2)

    ext = (cameras + 2 * reach) * rows
    blocks = pl.pallas_call(
        functools.partial(attend_kernel, reach),
        out_shape=[shape(planes, 4 * HD, rows)] * QUAD,
        in_specs=smem + vmem(3),
        out_specs=vmem(QUAD),
        scratch_shapes=[
            pltpu.VMEM((ext, HD), BF),
            pltpu.VMEM((ext, HD), BF),
            pltpu.VMEM((HD, ext), BF),
            pltpu.VMEM((HD, ext), BF),
            pltpu.VMEM((ext, HD), F32),
            pltpu.VMEM((ext, HD), F32),
            pltpu.VMEM((span, rows, 2 * rows), F32),
            pltpu.VMEM((span * rows, 2 * rows), BF),
            pltpu.VMEM((span * rows, 2 * rows), BF),
            pltpu.VMEM((cameras, HD, rows), BF),
            pltpu.VMEM((cameras, HD, rows), BF),
        ],
        compiler_params=params(32),
        name="attend",
    )(pos, bias, qk, vd)
    blocks = [blocks[0]] + [quad_swap(blocks[k], k) for k in range(1, QUAD)]

    terms = pl.pallas_call(
        functools.partial(weights_kernel, planes),
        out_shape=[shape(model // QUAD, 8 * HD)] * QUAD,
        in_specs=smem + vmem(QUAD + 2 * planes),
        out_specs=vmem(QUAD),
        scratch_shapes=[
            pltpu.VMEM((QUAD, planes, 4 * HD, rows), BF),
            pltpu.VMEM((6 * HD, 2 * planes * rows), BF),
            pltpu.VMEM((2 * HD, 2 * planes * rows), BF),
            pltpu.VMEM((2 * planes * rows, model), BF),
            pltpu.VMEM((2 * planes * rows, model), BF),
            pltpu.VMEM((model, 8 * HD), F32),
        ],
        compiler_params=params(32),
        name="weights",
    )(pos, *blocks, *own, *other)
    terms = [terms[0]] + [quad_swap(terms[k], k) for k in range(1, QUAD)]
    terms = pl.pallas_call(
        functools.partial(sum_kernel, planes),
        out_shape=[shape(model // cameras, 8 * HD)] * planes,
        in_specs=smem + vmem(QUAD),
        out_specs=vmem(planes),
        scratch_shapes=[pltpu.VMEM((model // QUAD, 8 * HD), F32)],
        compiler_params=params(16),
        name="plane_sum",
    )(pos, *terms)
    terms = [terms[0]] + [plane_swap(terms[k], k) for k in range(1, planes)]
    d_wqkv, d_wo = pl.pallas_call(
        functools.partial(finish_kernel, planes),
        out_shape=[shape(3, model // cameras, width, dtype=F32), shape(width, model // cameras, dtype=F32)],
        in_specs=smem + vmem(planes),
        out_specs=vmem(2),
        scratch_shapes=[pltpu.VMEM((planes, model // cameras, 8 * HD), F32)],
        compiler_params=params(16),
        name="finish",
    )(pos, *terms)

    stacked = jnp.stack([blocks[k] for k in range(QUAD)])
    order = quad ^ jnp.arange(QUAD)
    stacked = stacked[order][:, :, HD:]
    grads = []
    for k in range(planes):
        block = lax.dynamic_index_in_dim(stacked, plane ^ k, 1, keepdims=False)
        grads.append(block if k == 0 else plane_swap(block, k))
    mine, theirs = pl.pallas_call(
        functools.partial(inputs_kernel, planes),
        out_shape=[shape(scenes * rows, model // 2, dtype=F32)] * 2,
        in_specs=smem + vmem(planes + 1),
        out_specs=vmem(2),
        scratch_shapes=[
            pltpu.VMEM((planes, QUAD, 3 * HD, rows), BF),
            pltpu.VMEM((scenes, 3, width, rows), BF),
        ],
        compiler_params=params(32),
        name="inputs",
    )(pos, *grads, w_qkv)
    d_tokens = (mine + other_core(theirs)).astype(BF).reshape(scenes, 1, rows, model // 2)
    return (d_tokens, d_wqkv, d_wo)


def shifted(value, axis, steps):
    count = lax.axis_size(axis)
    pairs = [(source, (source + steps) % count) for source in range(count)]
    return lax.ppermute(value, axis, pairs)


def halo_body(tokens, queries, keys, values, w_qkv, w_out, d_out, neighbours, degrees):
    cameras = neighbours.shape[0]
    reach = neighbours.shape[1] // 2
    offsets = [step for step in range(-reach, reach + 1) if step != 0]
    camera = lax.axis_index("view")
    scenes, _, rows, width = queries.shape
    local_heads = width // HD
    scale = HD ** (-0.5)

    def split_heads(arr):
        return arr.reshape(scenes, rows, local_heads, HD)

    query = split_heads(queries)
    key_own = split_heads(keys)
    value_own = split_heads(values)
    d_flat = jnp.einsum(
        "std,ed->ste", d_out[:, 0], w_out, preferred_element_type=jnp.float32
    ).astype(jnp.bfloat16)
    d_heads = split_heads(d_flat)
    blocks = [(key_own, value_own, jnp.float32(1.0), 0)]
    for offset in offsets:
        key_far, value_far = shifted((keys, values), "view", -offset)
        listed = lax.dynamic_index_in_dim(neighbours, camera, 0, keepdims=False)
        count = lax.dynamic_index_in_dim(degrees, camera, 0, keepdims=False)
        target = (camera + offset) % cameras
        slots = jnp.arange(neighbours.shape[1], dtype=jnp.int32)
        hit = jnp.logical_and(listed == target, slots < count)
        blocks.append(
            (
                split_heads(key_far),
                split_heads(value_far),
                jnp.where(jnp.any(hit), 1.0, 0.0).astype(jnp.float32),
                offset,
            )
        )

    def block_scores(qry, key_blk):
        return (
            jnp.einsum("sthd,suhd->shtu", qry, key_blk, preferred_element_type=jnp.float32) * scale
        )

    top = jnp.full((scenes, local_heads, rows), -jnp.inf, jnp.float32)
    total = jnp.zeros((scenes, local_heads, rows), jnp.float32)
    for key_blk, value_blk, weight, offset in blocks:
        block = block_scores(query, key_blk)
        peak = jnp.where(weight > 0, jnp.max(block, axis=3), -jnp.inf)
        new_top = jnp.maximum(top, peak)
        factor = jnp.exp(top - new_top)
        prob = jnp.exp(block - new_top[..., None]) * weight
        total = total * factor + jnp.sum(prob, axis=3)
        top = new_top
    lse = top + jnp.log(total)
    accum = jnp.zeros((scenes, rows, local_heads, HD), jnp.float32)
    for key_blk, value_blk, weight, offset in blocks:
        prob_low = (jnp.exp(block_scores(query, key_blk) - lse[..., None]) * weight).astype(
            jnp.bfloat16
        )
        accum = accum + jnp.einsum(
            "shtu,suhd->sthd", prob_low, value_blk, preferred_element_type=jnp.float32
        )
    attended = accum.astype(jnp.bfloat16)
    delta = jnp.transpose(
        jnp.sum(d_heads.astype(jnp.float32) * attended.astype(jnp.float32), axis=3), (0, 2, 1)
    )

    def backward_block(qry, d_q, lse_blk, delta_blk, key_blk, value_blk, weight):
        block = block_scores(qry, key_blk)
        prob = jnp.exp(block - lse_blk[..., None]) * weight
        d_prob = jnp.einsum("sthd,suhd->shtu", d_q, value_blk, preferred_element_type=jnp.float32)
        d_score = (prob * (d_prob - delta_blk[..., None])).astype(jnp.bfloat16)
        d_key = (
            jnp.einsum("shtu,sthd->suhd", d_score, qry, preferred_element_type=jnp.float32) * scale
        )
        d_value = jnp.einsum(
            "shtu,sthd->suhd", prob.astype(jnp.bfloat16), d_q, preferred_element_type=jnp.float32
        )
        d_query = None
        d_query = (
            jnp.einsum("shtu,suhd->sthd", d_score, key_blk, preferred_element_type=jnp.float32)
            * scale
        )
        return (d_query, d_key, d_value)

    d_query = jnp.zeros(query.shape, jnp.float32)
    d_key = jnp.zeros(query.shape, jnp.float32)
    d_value = jnp.zeros(query.shape, jnp.float32)
    for key_blk, value_blk, weight, offset in blocks:
        part_query, part_key, part_value = backward_block(
            query, d_heads, lse, delta, key_blk, value_blk, weight
        )
        d_query = d_query + part_query
        if offset == 0:
            d_key = part_key
            d_value = part_value
        else:
            back_key, back_value = shifted((part_key, part_value), "view", offset)
            d_key = d_key + back_key
            d_value = d_value + back_value
    grads = (
        jnp.stack([d_query, d_key, d_value]).reshape(3, scenes, rows, width).astype(jnp.bfloat16)
    )
    token_terms = jnp.einsum("jste,jde->std", grads, w_qkv, preferred_element_type=jnp.float32)[
        :, None
    ]
    d_tokens = lax.psum_scatter(token_terms, "head", scatter_dimension=3, tiled=True).astype(
        jnp.bfloat16
    )
    attended_flat = attended.reshape(scenes, rows, width)
    wqkv_terms = jnp.einsum(
        "std,jste->jde", tokens[:, 0], grads, preferred_element_type=jnp.float32
    )
    wo_terms = jnp.einsum(
        "ste,std->ed", attended_flat, d_out[:, 0], preferred_element_type=jnp.float32
    )
    d_wqkv, d_wo = (
        lax.psum_scatter(wqkv_terms, "view", scatter_dimension=1, tiled=True),
        lax.psum_scatter(wo_terms, "view", scatter_dimension=1, tiled=True),
    )
    return (d_tokens, d_wqkv, d_wo)


def body(tokens, queries, keys, values, w_qkv, w_out, d_out, neighbours, degrees):
    args = (tokens, queries, keys, values, w_qkv, w_out, d_out, neighbours, degrees)
    scenes, _, rows, width = queries.shape
    cameras, reach = neighbours.shape[0], neighbours.shape[1] // 2
    fits = (
        scenes == 2
        and lax.axis_size("head") == 2
        and scenes * (width // HD) == cameras == lax.axis_size("view")
        and rows == LANE
        and cameras == QUAD * QUAD
        and cameras >= 2 * reach + 2
    )
    return split_body(*args) if fits else halo_body(*args)


def solution(mesh):
    return jax.shard_map(
        body,
        mesh=mesh,
        in_specs=(
            P(None, "view", None, None),
            P(None, "view", None, "head"),
            P(None, "view", None, "head"),
            P(None, "view", None, "head"),
            P(None, None, "head"),
            P("head", None),
            P(None, "view", None, None),
            P(),
            P(),
        ),
        out_specs=(P(None, "view", None, "head"), P(None, "view", "head"), P("head", "view")),
        check_vma=False,
    )
```

```python
import functools

import jax
import jax.numpy as jnp
from jax import lax
from jax.experimental import pallas as pl
from jax.experimental.pallas import tpu as pltpu
from jax.sharding import PartitionSpec as P

HD = 64
LANE = 128
QUAD = 4
BF = jnp.bfloat16
F32 = jnp.float32
MIB = 2**20
OFF = -1e30


def mul(a, b):
    return jnp.dot(a, b, preferred_element_type=F32)


def mul_nt(a, b):
    return lax.dot_general(a, b, (((1,), (1,)), ((), ())), preferred_element_type=F32)


def call(kernel, name, outs, args, scratch=(), mib=16, us=1, after=(), scalars=0, load=False):
    args, after = list(args), list(after)
    specs = [pl.BlockSpec(memory_space=pltpu.SMEM)] * scalars
    for arg in args[scalars:]:
        if load:
            specs.append(pl.BlockSpec(arg.shape, lambda i, rank=arg.ndim: (0,) * rank))
        else:
            specs.append(pl.BlockSpec(memory_space=pltpu.VMEM))
    out_specs = [pl.BlockSpec(memory_space=pltpu.VMEM)] * len(outs)

    def run(pos_ref, *refs):
        kernel(pos_ref, *refs[: len(args)], *refs[len(args) + len(after) :])

    return lambda pos: pl.pallas_call(
        run,
        out_shape=[jax.ShapeDtypeStruct(dims, dtype) for dims, dtype in outs],
        grid=(1,) if load else (),
        in_specs=[pl.BlockSpec(memory_space=pltpu.SMEM)] + specs + [pl.BlockSpec(memory_space=pl.ANY)] * len(after),
        out_specs=out_specs,
        scratch_shapes=[pltpu.VMEM(dims, dtype) for dims, dtype in scratch],
        compiler_params=pltpu.CompilerParams(vmem_limit_bytes=mib * MIB),
        cost_estimate=pl.CostEstimate(flops=int(us * 1.1e9), bytes_accessed=MIB, transcendentals=0),
        name=name,
    )(pos, *args, *after)


def pack_kernel(pos_ref, q_ref, k_ref, v_ref, d_ref, w_ref, out_ref):
    for scene in range(q_ref.shape[0]):
        arrays = (
            (q_ref[scene, 0].T * HD**-0.5).astype(BF),
            k_ref[scene, 0].T,
            v_ref[scene, 0].T,
            mul_nt(w_ref[...], d_ref[scene, 0]).astype(BF),
        )
        for view in range(out_ref.shape[0]):
            plane, quad = view // QUAD, view % QUAD
            if quad // 2 == scene:
                row = (2 * plane + quad % 2) * HD
                for n, arr in enumerate(arrays):
                    out_ref[view, n * HD : (n + 1) * HD] = arr[row : row + HD]


def fetch_kernel(pos_ref, t_ref, d_ref, both, t_out, d_out):
    core = pos_ref[2]
    both[:LANE] = t_out[...] = t_ref[core, 0]
    both[LANE:] = d_out[...] = d_ref[core, 0]


def gate(value, after):
    return lax.optimization_barrier((value, after))[0]


def cameras_of(pos_ref, planes):
    for j in range(QUAD):
        for k in range(planes):
            yield j, k, (pos_ref[0] ^ k) * QUAD + (pos_ref[1] ^ j)


def rows_of(cam):
    return pl.ds(pl.multiple_of(cam * LANE, LANE), LANE)


def wrap(ref, cameras, reach, by_lane):
    low, high, edge = reach * LANE, (cameras + reach) * LANE, reach * LANE
    if by_lane:
        ref[:, :edge] = ref[:, high - edge : high]
        ref[:, high:] = ref[:, low : low + edge]
    else:
        ref[:edge] = ref[high - edge : high]
        ref[high:] = ref[low : low + edge]


def fold(acc, cameras, reach):
    low, high, edge = reach * LANE, (cameras + reach) * LANE, reach * LANE
    acc[high - edge : high] += acc[:edge]
    acc[low : low + edge] += acc[high:]


def attend_kernel(reach, pos_ref, near_ref, count_ref, in_ref, *refs):
    outs, (k_row, v_row, k_col, v_col, dk_acc, dv_acc, s_buf, p_buf, d_buf, att_buf, dq_buf) = refs[:QUAD], refs[QUAD:]
    cameras = in_ref.shape[0]
    span = 2 * reach + 2
    for cam in range(cameras):
        rows = slice((cam + reach) * LANE, (cam + reach + 1) * LANE)
        key, val = in_ref[cam, HD : 2 * HD], in_ref[cam, 2 * HD : 3 * HD]
        k_col[:, rows] = key
        v_col[:, rows] = val
        k_row[rows, :] = key.T
        v_row[rows, :] = val.T
    for ref, by_lane in ((k_col, True), (v_col, True), (k_row, False), (v_row, False)):
        wrap(ref, cameras, reach, by_lane)
    dk_acc[...] = jnp.zeros_like(dk_acc)
    dv_acc[...] = jnp.zeros_like(dv_acc)

    def step(i, carry):
        def pair(n):
            rows = slice(n * HD, (n + 1) * HD)
            return jnp.concatenate([in_ref[2 * i, rows], in_ref[2 * i + 1, rows]], axis=1)

        q_col, d_col = pair(0), pair(3)
        q_rows = q_col.T
        place = lax.broadcasted_iota(jnp.int32, (16, 2 * LANE), 0)
        second = lax.broadcasted_iota(jnp.int32, (16, 2 * LANE), 1) >= LANE
        target = lax.rem(2 * i + place + (cameras - reach), cameras)
        live = target == jnp.where(second, 2 * i + 1, 2 * i)
        for m in range(2 * reach):
            first, other = [jnp.where(m < count_ref[2 * i + t], near_ref[2 * i + t, m], -1) for t in range(2)]
            live = live | (target == jnp.where(second, other, first))
        offset = place - reach - jnp.where(second, 1, 0)
        bias = jnp.where(live & (jnp.abs(offset) <= reach), 0.0, OFF)
        window = pl.ds(pl.multiple_of(2 * i * LANE, 2 * LANE), span * LANE)
        top = None
        for j in range(span):
            score = mul(k_row[rows_of(2 * i + j), :], q_col)
            s_buf[j] = score
            peak = jnp.max(score, axis=0, keepdims=True) + bias[j : j + 1]
            top = peak if top is None else jnp.maximum(top, peak)
        total = jnp.zeros((8, 2 * LANE), F32)
        for j in range(span):
            prob = jnp.exp(s_buf[j] + (bias[j : j + 1] - top))
            total = total + jnp.sum(prob.reshape(LANE // 8, 8, 2 * LANE), axis=0)
            p_buf[j * LANE : (j + 1) * LANE] = prob.astype(BF)
        inv = 1.0 / jnp.sum(total, axis=0, keepdims=True)
        att = (mul(v_col[:, window], p_buf[...]) * inv).astype(BF)
        d_wide = d_col.astype(F32)
        delta = jnp.sum(att.astype(F32) * d_wide, axis=0, keepdims=True) * inv
        d_low = (d_wide * inv).astype(BF)
        dv_acc[window, :] += mul(p_buf[...], d_low.T)
        for j in range(span):
            rows = slice(j * LANE, (j + 1) * LANE)
            d_prob = mul(v_row[rows_of(2 * i + j), :], d_low)
            d_buf[rows] = (p_buf[rows].astype(F32) * (d_prob - delta)).astype(BF)
        dk_acc[window, :] += mul(d_buf[...], q_rows)
        d_query = (mul(k_col[:, window], d_buf[...]) * HD**-0.5).astype(BF)
        for t in range(2):
            att_buf[2 * i + t] = att[:, t * LANE : (t + 1) * LANE]
            dq_buf[2 * i + t] = d_query[:, t * LANE : (t + 1) * LANE]
        return carry

    lax.fori_loop(0, cameras // 2, step, 0)
    fold(dk_acc, cameras, reach)
    fold(dv_acc, cameras, reach)
    for j, k, cam in cameras_of(pos_ref, cameras // QUAD):
        rows = rows_of(cam + reach)
        outs[j][k, :HD] = att_buf[cam]
        outs[j][k, HD : 2 * HD] = dv_acc[rows, :].T.astype(BF)
        outs[j][k, 2 * HD : 3 * HD] = dq_buf[cam]
        outs[j][k, 3 * HD :] = dk_acc[rows, :].T.astype(BF)


def hand_out(wide, outs, planes, pos_ref):
    part = wide.shape[0] // (QUAD * planes)
    for j in range(QUAD):
        for p in range(planes):
            rows = pl.ds(pl.multiple_of((p * QUAD + (pos_ref[1] ^ j)) * part, part), part)
            outs[j][p * part : (p + 1) * part] = wide[rows, :].astype(BF)


def weights_kernel(planes, pos_ref, *refs):
    blocks, (tok_ref, d_ref), far, outs = refs[:QUAD], refs[QUAD : QUAD + 2], refs[QUAD + 2 : -9], refs[-9:-5]
    left, left_o, tok, d_o, wide = refs[-5:]
    quad, core = pos_ref[1], pos_ref[2]
    for j in range(QUAD):
        scene, half = (quad ^ j) // 2, (quad ^ j) % 2
        for k in range(planes):
            at = rows_of(2 * k + (scene ^ core))
            left_o[pl.ds(pl.multiple_of(half * HD, HD), HD), at] = blocks[j][k, :HD]
            for n in range(3):
                row = pl.multiple_of((2 * n + half) * HD, HD)
                left[pl.ds(row, HD), at] = blocks[j][k, (n + 1) * HD : (n + 2) * HD]
    for n in range(2):
        at = slice(n * LANE, (n + 1) * LANE)
        tok[at] = tok_ref[core ^ n, 0]
        d_o[at] = d_ref[core ^ n, 0]
    for n, ref in enumerate(far[:2], 2):
        at = slice(n * LANE, (n + 1) * LANE)
        tok[at] = ref[:LANE]
        d_o[at] = ref[LANE:]
    for n, ref in enumerate(far[2:]):
        at = slice((n // 2 + 4) * LANE, (n // 2 + 5) * LANE)
        (d_o if n % 2 else tok)[at] = ref[...]
    wide[:, : 6 * HD] = mul(left[...], tok[...]).T
    wide[:, 6 * HD :] = mul(left_o[...], d_o[...]).T
    hand_out(wide, outs, planes, pos_ref)


def sum_kernel(planes, pos_ref, *refs):
    terms, outs, total = refs[:QUAD], refs[QUAD:-1], refs[-1]
    acc = terms[0][...].astype(F32)
    for term in terms[1:]:
        acc = acc + term[...].astype(F32)
    total[...] = acc
    part = total.shape[0] // planes
    for k in range(planes):
        rows = pl.ds(pl.multiple_of((pos_ref[0] ^ k) * part, part), part)
        outs[k][...] = total[rows, :].astype(BF)


def finish_kernel(planes, pos_ref, *refs):
    terms, (w_ref, o_ref, buf) = refs[:planes], refs[planes:]
    for k in range(planes):
        buf[pos_ref[0] ^ k] = terms[k][...].astype(F32)
    two = 2 * HD
    for p in range(planes):
        cols = slice(p * two, (p + 1) * two)
        o_ref[:, cols] = buf[p, :, 3 * two :]
        for place, j in enumerate((2, 0, 1)):
            w_ref[j, :, cols] = buf[p, :, place * two : (place + 1) * two]


def turn_kernel(planes, pos_ref, *refs):
    for k in range(1, planes):
        for j in range(QUAD):
            refs[QUAD + k - 1][j] = refs[j][k, HD:]


def inputs_kernel(planes, pos_ref, *refs):
    own, far, (w_ref, mine, theirs, turned) = refs[:QUAD], refs[QUAD : QUAD + planes - 1], refs[QUAD + planes - 1 :]
    plane, quad, core = pos_ref[0], pos_ref[1], pos_ref[2]
    for k in range(planes):
        for j in range(QUAD):
            block = own[j][0, HD:] if k == 0 else far[k - 1][j]
            scene, half = (quad ^ j) // 2, (quad ^ j) % 2
            row = pl.ds(pl.multiple_of((2 * (plane ^ k) + half) * HD, HD), HD)
            for place, n in enumerate((2, 0, 1)):
                turned[scene, n, row] = block[place * HD : (place + 1) * HD]
    left = [jnp.concatenate([turned[scene, j].T for scene in range(2)], axis=0) for j in range(3)]
    half = w_ref.shape[1] // 2
    for ref, who in ((theirs, 1 - core), (mine, core)):
        rows = pl.ds(pl.multiple_of(who * half, half), half)
        acc = mul_nt(left[0], w_ref[0, rows, :])
        for j in range(1, 3):
            acc = acc + mul_nt(left[j], w_ref[j, rows, :])
        ref[...] = acc


def split_body(tokens, queries, keys, values, w_qkv, w_out, d_out, neighbours, degrees):
    cameras = neighbours.shape[0]
    reach = neighbours.shape[1] // 2
    planes = cameras // QUAD
    scenes, _, rows, width = queries.shape
    model = tokens.shape[3]
    part = model // cameras
    view, core = lax.axis_index("view"), lax.axis_index("head")
    pos = jnp.stack([view // QUAD, view % QUAD, core]).astype(jnp.int32)
    span = 2 * reach + 2
    ext = (cameras + 2 * reach) * rows

    def along(value, pairs):
        return lax.ppermute(value, "view", pairs)

    def over_plane(values):
        return [values[0]] + [along(values[j], [(i, i ^ j) for i in range(cameras)]) for j in range(1, QUAD)]

    def over_column(values, first=0):
        return [
            value if k == 0 else along(value, [(i, i ^ (k * QUAD)) for i in range(cameras)])
            for k, value in enumerate(values, first)
        ]

    def other_core(value):
        return lax.ppermute(value, "head", [(0, 1), (1, 0)])

    piece = ((rows, model), BF)
    both, tok, out = call(fetch_kernel, "fetch", [((2 * rows, model), BF), piece, piece], (tokens, d_out))(pos)

    arrays = (queries, keys, values, d_out, w_out)
    packed = call(pack_kernel, "pack", [((cameras, 4 * HD, rows), BF)], arrays, load=True)(pos)[0]
    packed = lax.all_to_all(packed, "view", 0, 0, tiled=True)

    block = ((planes, 4 * HD, rows), BF)
    blocks = call(
        functools.partial(attend_kernel, reach), "attend", [block] * QUAD, (neighbours, degrees, packed),
        [
            ((ext, HD), BF), ((ext, HD), BF), ((HD, ext), BF), ((HD, ext), BF), ((ext, HD), F32), ((ext, HD), F32),
            ((span, rows, 2 * rows), F32), ((span * rows, 2 * rows), BF), ((span * rows, 2 * rows), BF),
            ((cameras, HD, rows), BF), ((cameras, HD, rows), BF),
        ],
        32, 13, scalars=2,
    )(pos)
    done = blocks[0]
    blocks = over_plane(blocks)
    near = over_column([both], 1)[0]
    pieces = [over_column([gate(tok, packed)], 2)[0], over_column([gate(out, packed)], 2)[0]]
    pieces += [over_column([gate(value, done)], 1)[0] for value in pieces]
    column = []
    for value in [near] + pieces:
        column += [value, other_core(value)]
    column = column[:2] + [column[2 + n] for n in (0, 2, 1, 3, 4, 6, 5, 7)]

    depth = 2 * planes * rows
    args = blocks + [tokens, d_out] + column
    terms = call(
        functools.partial(weights_kernel, planes), "weights", [((model // QUAD, 8 * HD), BF)] * QUAD, args,
        [((6 * HD, depth), BF), ((2 * HD, depth), BF), ((depth, model), BF), ((depth, model), BF), ((model, 8 * HD), F32)],
        32, 3,
    )(pos)
    started = terms[:1]
    terms = call(
        functools.partial(sum_kernel, planes), "plane_sum", [((part, 8 * HD), BF)] * planes, over_plane(terms),
        [((model // QUAD, 8 * HD), F32)],
    )(pos)
    terms = over_column(terms)
    d_wqkv, d_wo = call(
        functools.partial(finish_kernel, planes), "finish", [((3, part, width), F32), ((part, width), F32)], terms,
        [((planes, part, 8 * HD), F32)],
    )(pos)

    grads = call(
        functools.partial(turn_kernel, planes), "turn", [((QUAD, 3 * HD, rows), BF)] * (planes - 1), blocks
    )(pos)
    args = blocks + over_column(grads, 1) + [w_qkv]
    mine, theirs = call(
        functools.partial(inputs_kernel, planes), "inputs", [((scenes * rows, model // 2), F32)] * 2, args,
        [((scenes, 3, width, rows), BF)], 32, 2, after=started,
    )(pos)
    d_tokens = (mine + other_core(theirs)).astype(BF).reshape(scenes, 1, rows, model // 2)
    return (d_tokens, d_wqkv, d_wo.T)


def shifted(value, axis, steps):
    count = lax.axis_size(axis)
    pairs = [(source, (source + steps) % count) for source in range(count)]
    return lax.ppermute(value, axis, pairs)


def halo_body(tokens, queries, keys, values, w_qkv, w_out, d_out, neighbours, degrees):
    cameras = neighbours.shape[0]
    reach = neighbours.shape[1] // 2
    offsets = [step for step in range(-reach, reach + 1) if step != 0]
    camera = lax.axis_index("view")
    scenes, _, rows, width = queries.shape
    local_heads = width // HD
    scale = HD ** (-0.5)

    def split_heads(arr):
        return arr.reshape(scenes, rows, local_heads, HD)

    query = split_heads(queries)
    key_own = split_heads(keys)
    value_own = split_heads(values)
    d_flat = jnp.einsum(
        "std,ed->ste", d_out[:, 0], w_out, preferred_element_type=jnp.float32
    ).astype(jnp.bfloat16)
    d_heads = split_heads(d_flat)
    blocks = [(key_own, value_own, jnp.float32(1.0), 0)]
    for offset in offsets:
        key_far, value_far = shifted((keys, values), "view", -offset)
        listed = lax.dynamic_index_in_dim(neighbours, camera, 0, keepdims=False)
        count = lax.dynamic_index_in_dim(degrees, camera, 0, keepdims=False)
        target = (camera + offset) % cameras
        slots = jnp.arange(neighbours.shape[1], dtype=jnp.int32)
        hit = jnp.logical_and(listed == target, slots < count)
        blocks.append(
            (
                split_heads(key_far),
                split_heads(value_far),
                jnp.where(jnp.any(hit), 1.0, 0.0).astype(jnp.float32),
                offset,
            )
        )

    def block_scores(qry, key_blk):
        return (
            jnp.einsum("sthd,suhd->shtu", qry, key_blk, preferred_element_type=jnp.float32) * scale
        )

    top = jnp.full((scenes, local_heads, rows), -jnp.inf, jnp.float32)
    total = jnp.zeros((scenes, local_heads, rows), jnp.float32)
    for key_blk, value_blk, weight, offset in blocks:
        block = block_scores(query, key_blk)
        peak = jnp.where(weight > 0, jnp.max(block, axis=3), -jnp.inf)
        new_top = jnp.maximum(top, peak)
        factor = jnp.exp(top - new_top)
        prob = jnp.exp(block - new_top[..., None]) * weight
        total = total * factor + jnp.sum(prob, axis=3)
        top = new_top
    lse = top + jnp.log(total)
    accum = jnp.zeros((scenes, rows, local_heads, HD), jnp.float32)
    for key_blk, value_blk, weight, offset in blocks:
        prob_low = (jnp.exp(block_scores(query, key_blk) - lse[..., None]) * weight).astype(
            jnp.bfloat16
        )
        accum = accum + jnp.einsum(
            "shtu,suhd->sthd", prob_low, value_blk, preferred_element_type=jnp.float32
        )
    attended = accum.astype(jnp.bfloat16)
    delta = jnp.transpose(
        jnp.sum(d_heads.astype(jnp.float32) * attended.astype(jnp.float32), axis=3), (0, 2, 1)
    )

    def backward_block(qry, d_q, lse_blk, delta_blk, key_blk, value_blk, weight):
        block = block_scores(qry, key_blk)
        prob = jnp.exp(block - lse_blk[..., None]) * weight
        d_prob = jnp.einsum("sthd,suhd->shtu", d_q, value_blk, preferred_element_type=jnp.float32)
        d_score = (prob * (d_prob - delta_blk[..., None])).astype(jnp.bfloat16)
        d_key = (
            jnp.einsum("shtu,sthd->suhd", d_score, qry, preferred_element_type=jnp.float32) * scale
        )
        d_value = jnp.einsum(
            "shtu,sthd->suhd", prob.astype(jnp.bfloat16), d_q, preferred_element_type=jnp.float32
        )
        d_query = None
        d_query = (
            jnp.einsum("shtu,suhd->sthd", d_score, key_blk, preferred_element_type=jnp.float32)
            * scale
        )
        return (d_query, d_key, d_value)

    d_query = jnp.zeros(query.shape, jnp.float32)
    d_key = jnp.zeros(query.shape, jnp.float32)
    d_value = jnp.zeros(query.shape, jnp.float32)
    for key_blk, value_blk, weight, offset in blocks:
        part_query, part_key, part_value = backward_block(
            query, d_heads, lse, delta, key_blk, value_blk, weight
        )
        d_query = d_query + part_query
        if offset == 0:
            d_key = part_key
            d_value = part_value
        else:
            back_key, back_value = shifted((part_key, part_value), "view", offset)
            d_key = d_key + back_key
            d_value = d_value + back_value
    grads = (
        jnp.stack([d_query, d_key, d_value]).reshape(3, scenes, rows, width).astype(jnp.bfloat16)
    )
    token_terms = jnp.einsum("jste,jde->std", grads, w_qkv, preferred_element_type=jnp.float32)[
        :, None
    ]
    d_tokens = lax.psum_scatter(token_terms, "head", scatter_dimension=3, tiled=True).astype(
        jnp.bfloat16
    )
    attended_flat = attended.reshape(scenes, rows, width)
    wqkv_terms = jnp.einsum(
        "std,jste->jde", tokens[:, 0], grads, preferred_element_type=jnp.float32
    )
    wo_terms = jnp.einsum(
        "ste,std->ed", attended_flat, d_out[:, 0], preferred_element_type=jnp.float32
    )
    d_wqkv, d_wo = (
        lax.psum_scatter(wqkv_terms, "view", scatter_dimension=1, tiled=True),
        lax.psum_scatter(wo_terms, "view", scatter_dimension=1, tiled=True),
    )
    return (d_tokens, d_wqkv, d_wo)


def body(tokens, queries, keys, values, w_qkv, w_out, d_out, neighbours, degrees):
    args = (tokens, queries, keys, values, w_qkv, w_out, d_out, neighbours, degrees)
    scenes, _, rows, width = queries.shape
    cameras, reach = neighbours.shape[0], neighbours.shape[1] // 2
    fits = (
        scenes == 2
        and lax.axis_size("head") == 2
        and scenes * (width // HD) == cameras == lax.axis_size("view")
        and rows == LANE
        and cameras == QUAD * QUAD
        and cameras >= 2 * reach + 2
    )
    return split_body(*args) if fits else halo_body(*args)


def solution(mesh):
    return jax.shard_map(
        body,
        mesh=mesh,
        in_specs=(
            P(None, "view", None, None),
            P(None, "view", None, "head"),
            P(None, "view", None, "head"),
            P(None, "view", None, "head"),
            P(None, None, "head"),
            P("head", None),
            P(None, "view", None, None),
            P(),
            P(),
        ),
        out_specs=(P(None, "view", None, "head"), P(None, "view", "head"), P("head", "view")),
        check_vma=False,
    )
```

```python
import functools

import jax
import jax.numpy as jnp
from jax import lax
from jax.experimental import pallas as pl
from jax.experimental.pallas import tpu as pltpu
from jax.sharding import PartitionSpec as P

HD = 64
LANE = 128
QUAD = 4
BF = jnp.bfloat16
F32 = jnp.float32
MIB = 2**20
OFF = -1e30


def mul(a, b):
    return jnp.dot(a, b, preferred_element_type=F32)


def mul_nt(a, b):
    return lax.dot_general(a, b, (((1,), (1,)), ((), ())), preferred_element_type=F32)


def call(kernel, name, outs, args, scratch=(), mib=16, us=1, after=(), scalars=0, inputs=None, sems=0):
    args, after = list(args), list(after)
    specs = [pl.BlockSpec(memory_space=pltpu.SMEM)] * scalars
    for arg in args[scalars:]:
        specs.append(pl.BlockSpec(memory_space=inputs or pltpu.VMEM))
    out_specs = [pl.BlockSpec(memory_space=pltpu.VMEM)] * len(outs)

    def run(pos_ref, *refs):
        kernel(pos_ref, *refs[: len(args)], *refs[len(args) + len(after) :])

    return lambda pos: pl.pallas_call(
        run,
        out_shape=[jax.ShapeDtypeStruct(dims, dtype) for dims, dtype in outs],
        in_specs=[pl.BlockSpec(memory_space=pltpu.SMEM)] + specs + [pl.BlockSpec(memory_space=pl.ANY)] * len(after),
        out_specs=out_specs,
        scratch_shapes=[pltpu.VMEM(dims, dtype) for dims, dtype in scratch] + [pltpu.SemaphoreType.DMA(())] * sems,
        compiler_params=pltpu.CompilerParams(vmem_limit_bytes=mib * MIB),
        cost_estimate=pl.CostEstimate(flops=int(us * 1.1e9), bytes_accessed=MIB, transcendentals=0),
        name=name,
    )(pos, *args, *after)


def pack_kernel(pos_ref, *refs):
    far, out_ref, near, sems = refs[:5], refs[5], refs[6:11], refs[11:]
    copies = [pltpu.make_async_copy(*trio) for trio in zip(far, near, sems)]
    for copy in copies:
        copy.start()
    q_ref, k_ref, v_ref, d_ref, w_ref = near
    scenes = range(q_ref.shape[0])

    def put(n, scene, arr):
        for view in range(out_ref.shape[0]):
            plane, quad = view // QUAD, view % QUAD
            if quad // 2 == scene:
                row = (2 * plane + quad % 2) * HD
                out_ref[view, n * HD : (n + 1) * HD] = arr[row : row + HD]

    copies[0].wait()
    for scene in scenes:
        put(0, scene, (q_ref[scene, 0].T * HD**-0.5).astype(BF))
    copies[1].wait()
    for scene in scenes:
        put(1, scene, k_ref[scene, 0].T)
    copies[2].wait()
    for scene in scenes:
        put(2, scene, v_ref[scene, 0].T)
    copies[3].wait()
    copies[4].wait()
    for scene in scenes:
        put(3, scene, mul_nt(w_ref[...], d_ref[scene, 0]).astype(BF))


def fetch_kernel(pos_ref, t_ref, d_ref, both, t_out, d_out, *sems):
    copies = [
        pltpu.make_async_copy(ref.at[pos_ref[2], 0], out, sem)
        for ref, out, sem in zip((t_ref, d_ref), (t_out, d_out), sems)
    ]
    for n, (copy, out) in enumerate(zip(copies, (t_out, d_out))):
        copy.start()
    for n, (copy, out) in enumerate(zip(copies, (t_out, d_out))):
        copy.wait()
        both[n * LANE : (n + 1) * LANE] = out[...]


def gate(value, after):
    return lax.optimization_barrier((value, after))[0]


def places(refs, mine):
    if len(refs) == 1:
        return [(refs[0].at[n], n) for n in range(refs[0].shape[0])]
    return [(ref, mine ^ n) for n, ref in enumerate(refs)]


def rows_of(cam):
    return pl.ds(pl.multiple_of(cam * LANE, LANE), LANE)


def wrap(ref, cameras, reach, by_lane):
    low, high, edge = reach * LANE, (cameras + reach) * LANE, reach * LANE
    if by_lane:
        ref[:, :edge] = ref[:, high - edge : high]
        ref[:, high:] = ref[:, low : low + edge]
    else:
        ref[:edge] = ref[high - edge : high]
        ref[high:] = ref[low : low + edge]


def fold(acc, cameras, reach):
    low, high, edge = reach * LANE, (cameras + reach) * LANE, reach * LANE
    acc[high - edge : high] += acc[:edge]
    acc[low : low + edge] += acc[high:]


def attend_kernel(reach, pos_ref, near_ref, count_ref, in_ref, *refs):
    outs, (k_row, v_row, k_col, v_col, dk_acc, dv_acc, s_buf, p_buf, d_buf, att_buf, dq_buf) = refs[:4], refs[4:]
    cameras = in_ref.shape[0]
    span = 2 * reach + 2
    for cam in range(cameras):
        rows = slice((cam + reach) * LANE, (cam + reach + 1) * LANE)
        key, val = in_ref[cam, HD : 2 * HD], in_ref[cam, 2 * HD : 3 * HD]
        k_col[:, rows] = key
        v_col[:, rows] = val
        k_row[rows, :] = key.T
        v_row[rows, :] = val.T
    for ref, by_lane in ((k_col, True), (v_col, True), (k_row, False), (v_row, False)):
        wrap(ref, cameras, reach, by_lane)
    dk_acc[...] = jnp.zeros_like(dk_acc)
    dv_acc[...] = jnp.zeros_like(dv_acc)

    def step(i, carry):
        def pair(n):
            rows = slice(n * HD, (n + 1) * HD)
            return jnp.concatenate([in_ref[2 * i, rows], in_ref[2 * i + 1, rows]], axis=1)

        q_col, d_col = pair(0), pair(3)
        q_rows = q_col.T
        place = lax.broadcasted_iota(jnp.int32, (16, 2 * LANE), 0)
        second = lax.broadcasted_iota(jnp.int32, (16, 2 * LANE), 1) >= LANE
        target = lax.rem(2 * i + place + (cameras - reach), cameras)
        live = target == jnp.where(second, 2 * i + 1, 2 * i)
        for m in range(2 * reach):
            first, other = [jnp.where(m < count_ref[2 * i + t], near_ref[2 * i + t, m], -1) for t in range(2)]
            live = live | (target == jnp.where(second, other, first))
        offset = place - reach - jnp.where(second, 1, 0)
        bias = jnp.where(live & (jnp.abs(offset) <= reach), 0.0, OFF)
        window = pl.ds(pl.multiple_of(2 * i * LANE, 2 * LANE), span * LANE)
        top = None
        for j in range(span):
            score = mul(k_row[rows_of(2 * i + j), :], q_col)
            s_buf[j] = score
            peak = jnp.max(score, axis=0, keepdims=True) + bias[j : j + 1]
            top = peak if top is None else jnp.maximum(top, peak)
        total = jnp.zeros((8, 2 * LANE), F32)
        for j in range(span):
            prob = jnp.exp(s_buf[j] + (bias[j : j + 1] - top))
            total = total + jnp.sum(prob.reshape(LANE // 8, 8, 2 * LANE), axis=0)
            p_buf[j * LANE : (j + 1) * LANE] = prob.astype(BF)
        inv = 1.0 / jnp.sum(total, axis=0, keepdims=True)
        att = (mul(v_col[:, window], p_buf[...]) * inv).astype(BF)
        d_wide = d_col.astype(F32)
        delta = jnp.sum(att.astype(F32) * d_wide, axis=0, keepdims=True) * inv
        d_low = (d_wide * inv).astype(BF)
        dv_acc[window, :] += mul(p_buf[...], d_low.T)
        for j in range(span):
            rows = slice(j * LANE, (j + 1) * LANE)
            d_prob = mul(v_row[rows_of(2 * i + j), :], d_low)
            d_buf[rows] = (p_buf[rows].astype(F32) * (d_prob - delta)).astype(BF)
        dk_acc[window, :] += mul(d_buf[...], q_rows)
        d_query = (mul(k_col[:, window], d_buf[...]) * HD**-0.5).astype(BF)
        for t in range(2):
            att_buf[2 * i + t] = att[:, t * LANE : (t + 1) * LANE]
            dq_buf[2 * i + t] = d_query[:, t * LANE : (t + 1) * LANE]
        return carry

    lax.fori_loop(0, cameras // 2, step, 0)
    fold(dk_acc, cameras, reach)
    fold(dv_acc, cameras, reach)
    for ref, quad in places(outs, pos_ref[1]):
        for plane in range(cameras // QUAD):
            cam = plane * QUAD + quad
            rows = rows_of(cam + reach)
            ref[plane, :HD] = att_buf[cam]
            ref[plane, HD : 2 * HD] = dv_acc[rows, :].T.astype(BF)
            ref[plane, 2 * HD : 3 * HD] = dq_buf[cam]
            ref[plane, 3 * HD :] = dk_acc[rows, :].T.astype(BF)


def weights_kernel(planes, pos_ref, *refs):
    blocks, (tok_ref, d_ref), far, outs = refs[:4], refs[4:6], refs[6:16], refs[16:-5]
    left, left_o, tok, d_o, wide = refs[-5:]
    plane, core = pos_ref[0], pos_ref[2]
    for ref, quad in places(blocks, pos_ref[1]):
        scene, half = quad // 2, quad % 2
        for k in range(planes):
            at = rows_of(2 * k + (scene ^ core))
            block = ref.at[plane ^ k]
            left_o[pl.ds(pl.multiple_of(half * HD, HD), HD), at] = block[:HD]
            for n in range(3):
                row = pl.multiple_of((2 * n + half) * HD, HD)
                left[pl.ds(row, HD), at] = block[(n + 1) * HD : (n + 2) * HD]
    for n in range(2):
        at = slice(n * LANE, (n + 1) * LANE)
        tok[at] = tok_ref[core ^ n, 0]
        d_o[at] = d_ref[core ^ n, 0]
    for n, ref in enumerate(far[:2], 2):
        at = slice(n * LANE, (n + 1) * LANE)
        tok[at] = ref[:LANE]
        d_o[at] = ref[LANE:]
    for n, ref in enumerate(far[2:]):
        at = slice((n % 4 + 4) * LANE, (n % 4 + 5) * LANE)
        (d_o if n // 4 else tok)[at] = ref[...]
    wide[:, : 6 * HD] = mul(left[...], tok[...]).T
    wide[:, 6 * HD :] = mul(left_o[...], d_o[...]).T
    part = wide.shape[0] // (QUAD * planes)
    for ref, quad in places(outs, pos_ref[1]):
        for p in range(planes):
            rows = pl.ds(pl.multiple_of((p * QUAD + quad) * part, part), part)
            ref[p * part : (p + 1) * part] = wide[rows, :].astype(BF)


def sum_kernel(planes, pos_ref, *refs):
    terms, outs, total = refs[:4], refs[4:-1], refs[-1]
    acc = None
    for ref, _ in places(terms, 0):
        acc = ref[...].astype(F32) if acc is None else acc + ref[...].astype(F32)
    total[...] = acc
    part = total.shape[0] // planes
    for ref, plane in places(outs, pos_ref[0]):
        rows = pl.ds(pl.multiple_of(plane * part, part), part)
        ref[...] = total[rows, :].astype(BF)


def finish_kernel(planes, pos_ref, *refs):
    terms, (w_ref, o_ref, buf) = refs[:4], refs[4:]
    for ref, plane in places(terms, pos_ref[0]):
        buf[plane] = ref[...].astype(F32)
    two = 2 * HD
    for p in range(planes):
        cols = slice(p * two, (p + 1) * two)
        o_ref[:, cols] = buf[p, :, 3 * two :]
        for place, j in enumerate((2, 0, 1)):
            w_ref[j, :, cols] = buf[p, :, place * two : (place + 1) * two]


def turn_kernel(planes, pos_ref, *refs):
    blocks, outs = refs[:4], refs[4:]
    for ref, quad in places(blocks, pos_ref[1]):
        for n in range(planes):
            if len(outs) == 1:
                outs[0][n, quad] = ref[n, HD:]
            elif n:
                outs[n - 1][quad] = ref[pos_ref[0] ^ n, HD:]


def inputs_kernel(planes, pos_ref, *refs):
    blocks, far, (w_ref, mine, theirs, turned) = refs[:4], refs[4:7], refs[7:]
    plane, core = pos_ref[0], pos_ref[2]

    def put(block, home, quad):
        row = pl.ds(pl.multiple_of((2 * home + quad % 2) * HD, HD), HD)
        for place, n in enumerate((2, 0, 1)):
            turned[quad // 2, n, row] = block[place * HD : (place + 1) * HD]

    if len(far) == 1:
        for home in range(planes):
            for quad in range(QUAD):
                put(far[0][home, quad], home, quad)
    else:
        for ref, quad in places(blocks, pos_ref[1]):
            put(ref[plane, HD:], plane, quad)
        for k, ref in enumerate(far, 1):
            for quad in range(QUAD):
                put(ref[quad], plane ^ k, quad)
    left = [jnp.concatenate([turned[scene, j].T for scene in range(2)], axis=0) for j in range(3)]
    half = w_ref.shape[1] // 2
    for ref, who in ((theirs, 1 - core), (mine, core)):
        rows = pl.ds(pl.multiple_of(who * half, half), half)
        acc = mul_nt(left[0], w_ref[0, rows, :])
        for j in range(1, 3):
            acc = acc + mul_nt(left[j], w_ref[j, rows, :])
        ref[...] = acc


def split_body(tokens, queries, keys, values, w_qkv, w_out, d_out, neighbours, degrees):
    cameras = neighbours.shape[0]
    reach = neighbours.shape[1] // 2
    planes = cameras // QUAD
    scenes, _, rows, width = queries.shape
    model = tokens.shape[3]
    part = model // cameras
    view, core = lax.axis_index("view"), lax.axis_index("head")
    pos = jnp.stack([view // QUAD, view % QUAD, core]).astype(jnp.int32)
    span = 2 * reach + 2
    ext = (cameras + 2 * reach) * rows

    def along(value, pairs):
        return lax.ppermute(value, "view", pairs)

    def over_plane(values):
        if len(values) == 1:
            groups = [[p * QUAD + j for j in range(QUAD)] for p in range(planes)]
            return [lax.all_to_all(values[0], "view", 0, 0, axis_index_groups=groups, tiled=True)]
        return [values[0]] + [along(values[j], [(i, i ^ j) for i in range(cameras)]) for j in range(1, QUAD)]

    def over_column(values, first=0):
        if len(values) == 1 and values[0].shape[0] == planes:
            groups = [[p * QUAD + j for p in range(planes)] for j in range(QUAD)]
            return [lax.all_to_all(values[0], "view", 0, 0, axis_index_groups=groups, tiled=True)]
        return [
            value if k == 0 else along(value, [(i, i ^ (k * QUAD)) for i in range(cameras)])
            for k, value in enumerate(values, first)
        ]

    def other_core(value):
        return lax.ppermute(value, "head", [(0, 1), (1, 0)])

    arrays = (queries, keys, values, d_out, w_out)
    packed = call(
        pack_kernel, "pack", [((cameras, 4 * HD, rows), BF)], arrays, [(arr.shape, BF) for arr in arrays],
        56, inputs=pl.ANY, sems=len(arrays),
    )(pos)[0]
    packed = lax.all_to_all(packed, "view", 0, 0, tiled=True)

    own = call(fetch_kernel, "fetch", [((2 * rows, model), BF), ((rows, model), BF), ((rows, model), BF)], (tokens, d_out), (), 40, inputs=pl.ANY, sems=2)(pos)
    near = over_column([own[0]], 1)[0]
    column = [near, other_core(near)]

    blocks = call(
        functools.partial(attend_kernel, reach), "attend", [((planes, 4 * HD, rows), BF)] * QUAD, (neighbours, degrees, packed),
        [
            ((ext, HD), BF), ((ext, HD), BF), ((HD, ext), BF), ((HD, ext), BF), ((ext, HD), F32), ((ext, HD), F32),
            ((span, rows, 2 * rows), F32), ((span * rows, 2 * rows), BF), ((span * rows, 2 * rows), BF),
            ((cameras, HD, rows), BF), ((cameras, HD, rows), BF),
        ],
        32, 5, scalars=2, after=[],
    )(pos)
    done = blocks[0]
    blocks = over_plane(blocks)
    first = over_column([gate(own[1], packed)], 2)[0]
    second = over_column([gate(own[2], packed)], 2)[0]
    for far in (first, second):
        column += [far, other_core(far)]
        far = over_column([gate(far, done)], 1)[0]
        column += [far, other_core(far)]

    depth = 2 * planes * rows
    terms = call(
        functools.partial(weights_kernel, planes), "weights", [((model // QUAD, 8 * HD), BF)] * QUAD, blocks + [tokens, d_out] + column,
        [((6 * HD, depth), BF), ((2 * HD, depth), BF), ((depth, model), BF), ((depth, model), BF), ((model, 8 * HD), F32)],
        32, 3,
    )(pos)
    started = terms[:1]
    terms = call(
        functools.partial(sum_kernel, planes), "plane_sum", [((part, 8 * HD), BF)] * planes, over_plane(terms), [((model // QUAD, 8 * HD), F32)],
    )(pos)
    d_wqkv, d_wo = call(
        functools.partial(finish_kernel, planes), "finish", [((3, part, width), F32), ((part, width), F32)],
        over_column(terms), [((planes, part, 8 * HD), F32)],
    )(pos)

    grads = call(functools.partial(turn_kernel, planes), "turn", [((QUAD, 3 * HD, rows), BF)] * (planes - 1), blocks, after=())(pos)
    args = blocks + over_column(grads, 1) + [w_qkv]
    mine, theirs = call(
        functools.partial(inputs_kernel, planes), "inputs", [((scenes * rows, model // 2), F32)] * 2, args,
        [((scenes, 3, width, rows), BF)], 32, 2, after=started,
    )(pos)
    d_tokens = (mine + other_core(theirs)).astype(BF).reshape(scenes, 1, rows, model // 2)
    return (d_tokens, d_wqkv, d_wo.T)


def shifted(value, axis, steps):
    count = lax.axis_size(axis)
    pairs = [(source, (source + steps) % count) for source in range(count)]
    return lax.ppermute(value, axis, pairs)


def halo_body(tokens, queries, keys, values, w_qkv, w_out, d_out, neighbours, degrees):
    cameras = neighbours.shape[0]
    reach = neighbours.shape[1] // 2
    offsets = [step for step in range(-reach, reach + 1) if step != 0]
    camera = lax.axis_index("view")
    scenes, _, rows, width = queries.shape
    local_heads = width // HD
    scale = HD ** (-0.5)

    def split_heads(arr):
        return arr.reshape(scenes, rows, local_heads, HD)

    query = split_heads(queries)
    key_own = split_heads(keys)
    value_own = split_heads(values)
    d_flat = jnp.einsum(
        "std,ed->ste", d_out[:, 0], w_out, preferred_element_type=jnp.float32
    ).astype(jnp.bfloat16)
    d_heads = split_heads(d_flat)
    blocks = [(key_own, value_own, jnp.float32(1.0), 0)]
    for offset in offsets:
        key_far, value_far = shifted((keys, values), "view", -offset)
        listed = lax.dynamic_index_in_dim(neighbours, camera, 0, keepdims=False)
        count = lax.dynamic_index_in_dim(degrees, camera, 0, keepdims=False)
        target = (camera + offset) % cameras
        slots = jnp.arange(neighbours.shape[1], dtype=jnp.int32)
        hit = jnp.logical_and(listed == target, slots < count)
        blocks.append(
            (
                split_heads(key_far),
                split_heads(value_far),
                jnp.where(jnp.any(hit), 1.0, 0.0).astype(jnp.float32),
                offset,
            )
        )

    def block_scores(qry, key_blk):
        return (
            jnp.einsum("sthd,suhd->shtu", qry, key_blk, preferred_element_type=jnp.float32) * scale
        )

    top = jnp.full((scenes, local_heads, rows), -jnp.inf, jnp.float32)
    total = jnp.zeros((scenes, local_heads, rows), jnp.float32)
    for key_blk, value_blk, weight, offset in blocks:
        block = block_scores(query, key_blk)
        peak = jnp.where(weight > 0, jnp.max(block, axis=3), -jnp.inf)
        new_top = jnp.maximum(top, peak)
        factor = jnp.exp(top - new_top)
        prob = jnp.exp(block - new_top[..., None]) * weight
        total = total * factor + jnp.sum(prob, axis=3)
        top = new_top
    lse = top + jnp.log(total)
    accum = jnp.zeros((scenes, rows, local_heads, HD), jnp.float32)
    for key_blk, value_blk, weight, offset in blocks:
        prob_low = (jnp.exp(block_scores(query, key_blk) - lse[..., None]) * weight).astype(
            jnp.bfloat16
        )
        accum = accum + jnp.einsum(
            "shtu,suhd->sthd", prob_low, value_blk, preferred_element_type=jnp.float32
        )
    attended = accum.astype(jnp.bfloat16)
    delta = jnp.transpose(
        jnp.sum(d_heads.astype(jnp.float32) * attended.astype(jnp.float32), axis=3), (0, 2, 1)
    )

    def backward_block(qry, d_q, lse_blk, delta_blk, key_blk, value_blk, weight):
        block = block_scores(qry, key_blk)
        prob = jnp.exp(block - lse_blk[..., None]) * weight
        d_prob = jnp.einsum("sthd,suhd->shtu", d_q, value_blk, preferred_element_type=jnp.float32)
        d_score = (prob * (d_prob - delta_blk[..., None])).astype(jnp.bfloat16)
        d_key = (
            jnp.einsum("shtu,sthd->suhd", d_score, qry, preferred_element_type=jnp.float32) * scale
        )
        d_value = jnp.einsum(
            "shtu,sthd->suhd", prob.astype(jnp.bfloat16), d_q, preferred_element_type=jnp.float32
        )
        d_query = None
        d_query = (
            jnp.einsum("shtu,suhd->sthd", d_score, key_blk, preferred_element_type=jnp.float32)
            * scale
        )
        return (d_query, d_key, d_value)

    d_query = jnp.zeros(query.shape, jnp.float32)
    d_key = jnp.zeros(query.shape, jnp.float32)
    d_value = jnp.zeros(query.shape, jnp.float32)
    for key_blk, value_blk, weight, offset in blocks:
        part_query, part_key, part_value = backward_block(
            query, d_heads, lse, delta, key_blk, value_blk, weight
        )
        d_query = d_query + part_query
        if offset == 0:
            d_key = part_key
            d_value = part_value
        else:
            back_key, back_value = shifted((part_key, part_value), "view", offset)
            d_key = d_key + back_key
            d_value = d_value + back_value
    grads = (
        jnp.stack([d_query, d_key, d_value]).reshape(3, scenes, rows, width).astype(jnp.bfloat16)
    )
    token_terms = jnp.einsum("jste,jde->std", grads, w_qkv, preferred_element_type=jnp.float32)[
        :, None
    ]
    d_tokens = lax.psum_scatter(token_terms, "head", scatter_dimension=3, tiled=True).astype(
        jnp.bfloat16
    )
    attended_flat = attended.reshape(scenes, rows, width)
    wqkv_terms = jnp.einsum(
        "std,jste->jde", tokens[:, 0], grads, preferred_element_type=jnp.float32
    )
    wo_terms = jnp.einsum(
        "ste,std->ed", attended_flat, d_out[:, 0], preferred_element_type=jnp.float32
    )
    d_wqkv, d_wo = (
        lax.psum_scatter(wqkv_terms, "view", scatter_dimension=1, tiled=True),
        lax.psum_scatter(wo_terms, "view", scatter_dimension=1, tiled=True),
    )
    return (d_tokens, d_wqkv, d_wo)


def body(tokens, queries, keys, values, w_qkv, w_out, d_out, neighbours, degrees):
    args = (tokens, queries, keys, values, w_qkv, w_out, d_out, neighbours, degrees)
    scenes, _, rows, width = queries.shape
    cameras, reach = neighbours.shape[0], neighbours.shape[1] // 2
    fits = (
        scenes == 2
        and lax.axis_size("head") == 2
        and scenes * (width // HD) == cameras == lax.axis_size("view")
        and rows == LANE
        and cameras == QUAD * QUAD
        and cameras >= 2 * reach + 2
    )
    return split_body(*args) if fits else halo_body(*args)


def solution(mesh):
    return jax.shard_map(
        body,
        mesh=mesh,
        in_specs=(
            P(None, "view", None, None),
            P(None, "view", None, "head"),
            P(None, "view", None, "head"),
            P(None, "view", None, "head"),
            P(None, None, "head"),
            P("head", None),
            P(None, "view", None, None),
            P(),
            P(),
        ),
        out_specs=(P(None, "view", None, "head"), P(None, "view", "head"), P("head", "view")),
        check_vma=False,
    )
```

```python
import functools

import jax
import jax.numpy as jnp
from jax import lax
from jax.experimental import pallas as pl
from jax.experimental.pallas import tpu as pltpu
from jax.sharding import PartitionSpec as P

HD = 64
LANE = 128
QUAD = 4
BF = jnp.bfloat16
F32 = jnp.float32
MIB = 2**20
OFF = -1e30


def mul(a, b):
    return jnp.dot(a, b, preferred_element_type=F32)


def mul_nt(a, b):
    return lax.dot_general(a, b, (((1,), (1,)), ((), ())), preferred_element_type=F32)


def call(kernel, name, outs, args, scratch=(), mib=16, us=1, after=(), scalars=0, inputs=None, sems=0):
    args, after = list(args), list(after)
    specs = [pl.BlockSpec(memory_space=pltpu.SMEM)] * scalars
    for arg in args[scalars:]:
        specs.append(pl.BlockSpec(memory_space=inputs or pltpu.VMEM))
    out_specs = [pl.BlockSpec(memory_space=pltpu.VMEM)] * len(outs)

    def run(pos_ref, *refs):
        kernel(pos_ref, *refs[: len(args)], *refs[len(args) + len(after) :])

    return lambda pos: pl.pallas_call(
        run,
        out_shape=[jax.ShapeDtypeStruct(dims, dtype) for dims, dtype in outs],
        in_specs=[pl.BlockSpec(memory_space=pltpu.SMEM)] + specs + [pl.BlockSpec(memory_space=pl.ANY)] * len(after),
        out_specs=out_specs,
        scratch_shapes=[pltpu.VMEM(dims, dtype) for dims, dtype in scratch] + [pltpu.SemaphoreType.DMA(())] * sems,
        compiler_params=pltpu.CompilerParams(vmem_limit_bytes=mib * MIB),
        cost_estimate=pl.CostEstimate(flops=int(us * 1.1e9), bytes_accessed=MIB, transcendentals=0),
        name=name,
    )(pos, *args, *after)


def pack_kernel(_, *refs):
    far, out_ref, near, sems = refs[:5], refs[5], refs[6:11], refs[11:]
    copies = [pltpu.make_async_copy(*trio) for trio in zip(far, near, sems)]
    for copy in copies:
        copy.start()
    q_ref, k_ref, v_ref, d_ref, w_ref = near
    scenes = range(q_ref.shape[0])

    def put(n, scene, arr):
        for view in range(out_ref.shape[0]):
            plane, quad = view // QUAD, view % QUAD
            if quad // 2 == scene:
                row = (2 * plane + quad % 2) * HD
                out_ref[view, n * HD : (n + 1) * HD] = arr[row : row + HD]

    copies[0].wait()
    for scene in scenes:
        put(0, scene, (q_ref[scene, 0].T * HD**-0.5).astype(BF))
    copies[1].wait()
    for scene in scenes:
        put(1, scene, k_ref[scene, 0].T)
    copies[2].wait()
    for scene in scenes:
        put(2, scene, v_ref[scene, 0].T)
    copies[3].wait()
    copies[4].wait()
    d_head = mul_nt(w_ref[...], d_ref[...].reshape(len(scenes) * LANE, -1)).astype(BF)
    for scene in scenes:
        put(3, scene, d_head[:, scene * LANE : (scene + 1) * LANE])


def fetch_kernel(pos_ref, t_ref, d_ref, both, t_out, d_out, *sems):
    copies = [
        pltpu.make_async_copy(ref.at[pos_ref[2], 0], out, sem)
        for ref, out, sem in zip((t_ref, d_ref), (t_out, d_out), sems)
    ]
    for n, (copy, out) in enumerate(zip(copies, (t_out, d_out))):
        copy.start()
    for n, (copy, out) in enumerate(zip(copies, (t_out, d_out))):
        copy.wait()
        both[n * LANE : (n + 1) * LANE] = out[...]


def gate(value, after):
    return lax.optimization_barrier((value, after))[0]


def places(refs, mine):
    if len(refs) == 1:
        return [(refs[0].at[n], n) for n in range(refs[0].shape[0])]
    return [(ref, mine ^ n) for n, ref in enumerate(refs)]


def rows_of(cam):
    return pl.ds(pl.multiple_of(cam * LANE, LANE), LANE)


def wrap(ref, cameras, reach, by_lane):
    low, high, edge = reach * LANE, (cameras + reach) * LANE, reach * LANE
    if by_lane:
        ref[:, :edge] = ref[:, high - edge : high]
        ref[:, high:] = ref[:, low : low + edge]
    else:
        ref[:edge] = ref[high - edge : high]
        ref[high:] = ref[low : low + edge]


def fold(acc, cameras, reach):
    low, high, edge = reach * LANE, (cameras + reach) * LANE, reach * LANE
    acc[high - edge : high] += acc[:edge]
    acc[low : low + edge] += acc[high:]


def attend_kernel(reach, pos_ref, near_ref, count_ref, in_ref, *refs):
    outs, (k_row, v_row, k_col, v_col, dk_acc, dv_acc, s_buf, p_buf, d_buf, att_buf, dq_buf) = refs[:4], refs[4:]
    cameras = in_ref.shape[0]
    span = 2 * reach + 2
    for cam in range(cameras):
        rows = slice((cam + reach) * LANE, (cam + reach + 1) * LANE)
        key, val = in_ref[cam, HD : 2 * HD], in_ref[cam, 2 * HD : 3 * HD]
        k_col[:, rows] = key
        v_col[:, rows] = val
        k_row[rows, :] = key.T
        v_row[rows, :] = val.T
    for ref, by_lane in ((k_col, True), (v_col, True), (k_row, False), (v_row, False)):
        wrap(ref, cameras, reach, by_lane)
    dk_acc[...] = jnp.zeros_like(dk_acc)
    dv_acc[...] = jnp.zeros_like(dv_acc)

    def step(i, carry):
        def pair(n):
            rows = slice(n * HD, (n + 1) * HD)
            return jnp.concatenate([in_ref[2 * i, rows], in_ref[2 * i + 1, rows]], axis=1)

        q_col, d_col = pair(0), pair(3)
        q_rows = q_col.T
        place = lax.broadcasted_iota(jnp.int32, (16, 2 * LANE), 0)
        second = lax.broadcasted_iota(jnp.int32, (16, 2 * LANE), 1) >= LANE
        target = lax.rem(2 * i + place + (cameras - reach), cameras)
        live = target == jnp.where(second, 2 * i + 1, 2 * i)
        for m in range(2 * reach):
            first, other = [jnp.where(m < count_ref[2 * i + t], near_ref[2 * i + t, m], -1) for t in range(2)]
            live = live | (target == jnp.where(second, other, first))
        offset = place - reach - jnp.where(second, 1, 0)
        bias = jnp.where(live & (jnp.abs(offset) <= reach), 0.0, OFF)
        window = pl.ds(pl.multiple_of(2 * i * LANE, 2 * LANE), span * LANE)
        top = None
        for j in range(span):
            score = mul(k_row[rows_of(2 * i + j), :], q_col)
            s_buf[j] = score
            peak = jnp.max(score, axis=0, keepdims=True) + bias[j : j + 1]
            top = peak if top is None else jnp.maximum(top, peak)
        total = jnp.zeros((8, 2 * LANE), F32)
        for j in range(span):
            prob = jnp.exp(s_buf[j] + (bias[j : j + 1] - top))
            total = total + jnp.sum(prob.reshape(LANE // 8, 8, 2 * LANE), axis=0)
            p_buf[j * LANE : (j + 1) * LANE] = prob.astype(BF)
        inv = 1.0 / jnp.sum(total, axis=0, keepdims=True)
        att = (mul(v_col[:, window], p_buf[...]) * inv).astype(BF)
        d_wide = d_col.astype(F32)
        delta = jnp.sum(att.astype(F32) * d_wide, axis=0, keepdims=True) * inv
        d_low = (d_wide * inv).astype(BF)
        dv_acc[window, :] += mul(p_buf[...], d_low.T)
        for j in range(span):
            rows = slice(j * LANE, (j + 1) * LANE)
            d_prob = mul(v_row[rows_of(2 * i + j), :], d_low)
            d_buf[rows] = (p_buf[rows].astype(F32) * (d_prob - delta)).astype(BF)
        dk_acc[window, :] += mul(d_buf[...], q_rows)
        d_query = (mul(k_col[:, window], d_buf[...]) * HD**-0.5).astype(BF)
        for t in range(2):
            att_buf[2 * i + t] = att[:, t * LANE : (t + 1) * LANE]
            dq_buf[2 * i + t] = d_query[:, t * LANE : (t + 1) * LANE]
        return carry

    lax.fori_loop(0, cameras // 2, step, 0)
    fold(dk_acc, cameras, reach)
    fold(dv_acc, cameras, reach)
    for ref, quad in places(outs, pos_ref[1]):
        for plane in range(cameras // QUAD):
            cam = plane * QUAD + quad
            rows = rows_of(cam + reach)
            ref[plane, :HD] = att_buf[cam]
            ref[plane, HD : 2 * HD] = dv_acc[rows, :].T.astype(BF)
            ref[plane, 2 * HD : 3 * HD] = dq_buf[cam]
            ref[plane, 3 * HD :] = dk_acc[rows, :].T.astype(BF)


def weights_kernel(planes, pos_ref, *refs):
    blocks, (tok_ref, d_ref), far, outs = refs[:4], refs[4:6], refs[6:16], refs[16:-5]
    left, left_o, tok, d_o, wide = refs[-5:]
    plane, core = pos_ref[0], pos_ref[2]
    for ref, quad in places(blocks, pos_ref[1]):
        scene, half = quad // 2, quad % 2
        for k in range(planes):
            at = rows_of(2 * k + (scene ^ core))
            block = ref.at[plane ^ k]
            left_o[pl.ds(pl.multiple_of(half * HD, HD), HD), at] = block[:HD]
            for n in range(3):
                row = pl.multiple_of((2 * n + half) * HD, HD)
                left[pl.ds(row, HD), at] = block[(n + 1) * HD : (n + 2) * HD]
    for n in range(2):
        at = slice(n * LANE, (n + 1) * LANE)
        tok[at] = tok_ref[core ^ n, 0]
        d_o[at] = d_ref[core ^ n, 0]
    for n, ref in enumerate(far[:2], 2):
        at = slice(n * LANE, (n + 1) * LANE)
        tok[at] = ref[:LANE]
        d_o[at] = ref[LANE:]
    for n, ref in enumerate(far[2:]):
        at = slice((n % 4 + 4) * LANE, (n % 4 + 5) * LANE)
        (d_o if n // 4 else tok)[at] = ref[...]
    wide[:, : 6 * HD] = mul(left[...], tok[...]).astype(BF).T
    wide[:, 6 * HD :] = mul(left_o[...], d_o[...]).astype(BF).T
    part = wide.shape[0] // (QUAD * planes)
    for ref, quad in places(outs, pos_ref[1]):
        for p in range(planes):
            rows = pl.ds(pl.multiple_of((p * QUAD + quad) * part, part), part)
            ref[p * part : (p + 1) * part] = wide[rows, :]


def sum_kernel(planes, pos_ref, *refs):
    terms, outs = refs[:QUAD], refs[QUAD:]
    part = terms[0].shape[0] // planes
    for ref, plane in places(outs, pos_ref[0]):
        rows = pl.ds(pl.multiple_of(plane * part, part), part)
        acc = terms[0][rows, :].astype(F32)
        for term in terms[1:]:
            acc = acc + term[rows, :].astype(F32)
        ref[...] = acc.astype(BF)


def finish_kernel(planes, pos_ref, *refs):
    terms, (w_ref, o_ref) = refs[:planes], refs[planes:]
    two = 2 * HD
    for ref, plane in places(terms, pos_ref[0]):
        cols = pl.ds(pl.multiple_of(plane * two, two), two)
        o_ref[:, cols] = ref[:, 3 * two :].astype(F32)
        for place, j in enumerate((2, 0, 1)):
            w_ref[j, :, cols] = ref[:, place * two : (place + 1) * two].astype(F32)


def turn_kernel(planes, pos_ref, *refs):
    blocks, outs = refs[:4], refs[4:]
    for ref, quad in places(blocks, pos_ref[1]):
        for n in range(planes):
            if len(outs) == 1:
                outs[0][n, quad] = ref[n, HD:]
            elif n:
                outs[n - 1][quad] = ref[pos_ref[0] ^ n, HD:]


def inputs_kernel(planes, pos_ref, *refs):
    blocks, far, (w_ref, mine, theirs, turned) = refs[:4], refs[4:7], refs[7:]
    plane, core = pos_ref[0], pos_ref[2]

    def put(block, home, quad):
        row = pl.ds(pl.multiple_of((2 * home + quad % 2) * HD, HD), HD)
        for place, n in enumerate((2, 0, 1)):
            turned[quad // 2, n, row] = block[place * HD : (place + 1) * HD]

    if len(far) == 1:
        for home in range(planes):
            for quad in range(QUAD):
                put(far[0][home, quad], home, quad)
    else:
        for ref, quad in places(blocks, pos_ref[1]):
            put(ref[plane, HD:], plane, quad)
        for k, ref in enumerate(far, 1):
            for quad in range(QUAD):
                put(ref[quad], plane ^ k, quad)
    left = [jnp.concatenate([turned[scene, j].T for scene in range(2)], axis=0) for j in range(3)]
    half = w_ref.shape[1] // 2
    for ref, who in ((theirs, 1 - core), (mine, core)):
        rows = pl.ds(pl.multiple_of(who * half, half), half)
        acc = mul_nt(left[0], w_ref[0, rows, :])
        for j in range(1, 3):
            acc = acc + mul_nt(left[j], w_ref[j, rows, :])
        ref[...] = acc


def split_body(tokens, queries, keys, values, w_qkv, w_out, d_out, neighbours, degrees):
    cameras = neighbours.shape[0]
    reach = neighbours.shape[1] // 2
    planes = cameras // QUAD
    scenes, _, rows, width = queries.shape
    model = tokens.shape[3]
    part = model // cameras
    view, core = lax.axis_index("view"), lax.axis_index("head")
    pos = jnp.stack([view // QUAD, view % QUAD, core]).astype(jnp.int32)
    span = 2 * reach + 2
    ext = (cameras + 2 * reach) * rows

    def along(value, pairs):
        return lax.ppermute(value, "view", pairs)

    def over_plane(values):
        if len(values) == 1:
            groups = [[p * QUAD + j for j in range(QUAD)] for p in range(planes)]
            return [lax.all_to_all(values[0], "view", 0, 0, axis_index_groups=groups, tiled=True)]
        return [values[0]] + [along(values[j], [(i, i ^ j) for i in range(cameras)]) for j in range(1, QUAD)]

    def over_column(values, first=0):
        if len(values) == 1 and values[0].shape[0] == planes:
            groups = [[p * QUAD + j for p in range(planes)] for j in range(QUAD)]
            return [lax.all_to_all(values[0], "view", 0, 0, axis_index_groups=groups, tiled=True)]
        return [
            value if k == 0 else along(value, [(i, i ^ (k * QUAD)) for i in range(cameras)])
            for k, value in enumerate(values, first)
        ]

    def other_core(value):
        return lax.ppermute(value, "head", [(0, 1), (1, 0)])

    arrays = (queries, keys, values, d_out, w_out)
    packed = call(
        pack_kernel, "pack", [((cameras, 4 * HD, rows), BF)], arrays, [(arr.shape, BF) for arr in arrays],
        56, inputs=pl.ANY, sems=len(arrays),
    )(jnp.zeros(1, jnp.int32))[0]
    packed = lax.all_to_all(packed, "view", 0, 0, tiled=True)

    own = call(fetch_kernel, "fetch", [((2 * rows, model), BF), ((rows, model), BF), ((rows, model), BF)], (tokens, d_out), (), 40, inputs=pl.ANY, sems=2)(pos)
    near = over_column([own[0]], 1)[0]
    column = [near, other_core(near)]

    blocks = call(
        functools.partial(attend_kernel, reach), "attend", [((planes, 4 * HD, rows), BF)] * QUAD, (neighbours, degrees, packed),
        [
            ((ext, HD), BF), ((ext, HD), BF), ((HD, ext), BF), ((HD, ext), BF), ((ext, HD), F32), ((ext, HD), F32),
            ((span, rows, 2 * rows), F32), ((span * rows, 2 * rows), BF), ((span * rows, 2 * rows), BF),
            ((cameras, HD, rows), BF), ((cameras, HD, rows), BF),
        ],
        32, 5, scalars=2, after=[],
    )(pos)
    done = blocks[0]
    blocks = over_plane(blocks)
    first = over_column([gate(own[1], packed)], 2)[0]
    second = over_column([gate(own[2], packed)], 2)[0]
    for far in (first, second):
        column += [far, other_core(far)]
        far = over_column([gate(far, done)], 1)[0]
        column += [far, other_core(far)]

    depth = 2 * planes * rows
    terms = call(
        functools.partial(weights_kernel, planes), "weights", [((model // QUAD, 8 * HD), BF)] * QUAD, blocks + [tokens, d_out] + column,
        [((6 * HD, depth), BF), ((2 * HD, depth), BF), ((depth, model), BF), ((depth, model), BF), ((model, 8 * HD), BF)],
        32, 3,
    )(pos)
    started = terms[:1]
    terms = call(
        functools.partial(sum_kernel, planes), "plane_sum", [((part, 8 * HD), BF)] * planes, over_plane(terms),
    )(pos)
    d_wqkv, d_wo = call(
        functools.partial(finish_kernel, planes), "finish", [((3, part, width), F32), ((part, width), F32)],
        over_column(terms),
    )(pos)

    grads = call(functools.partial(turn_kernel, planes), "turn", [((QUAD, 3 * HD, rows), BF)] * (planes - 1), blocks, after=())(pos)
    args = blocks + over_column(grads, 1) + [w_qkv]
    mine, theirs = call(
        functools.partial(inputs_kernel, planes), "inputs", [((scenes * rows, model // 2), F32)] * 2, args,
        [((scenes, 3, width, rows), BF)], 32, 2, after=started,
    )(pos)
    d_tokens = (mine + other_core(theirs)).astype(BF).reshape(scenes, 1, rows, model // 2)
    return (d_tokens, d_wqkv, d_wo.T)


def shifted(value, axis, steps):
    count = lax.axis_size(axis)
    pairs = [(source, (source + steps) % count) for source in range(count)]
    return lax.ppermute(value, axis, pairs)


def halo_body(tokens, queries, keys, values, w_qkv, w_out, d_out, neighbours, degrees):
    cameras = neighbours.shape[0]
    reach = neighbours.shape[1] // 2
    offsets = [step for step in range(-reach, reach + 1) if step != 0]
    camera = lax.axis_index("view")
    scenes, _, rows, width = queries.shape
    local_heads = width // HD
    scale = HD ** (-0.5)

    def split_heads(arr):
        return arr.reshape(scenes, rows, local_heads, HD)

    query = split_heads(queries)
    key_own = split_heads(keys)
    value_own = split_heads(values)
    d_flat = jnp.einsum(
        "std,ed->ste", d_out[:, 0], w_out, preferred_element_type=jnp.float32
    ).astype(jnp.bfloat16)
    d_heads = split_heads(d_flat)
    blocks = [(key_own, value_own, jnp.float32(1.0), 0)]
    for offset in offsets:
        key_far, value_far = shifted((keys, values), "view", -offset)
        listed = lax.dynamic_index_in_dim(neighbours, camera, 0, keepdims=False)
        count = lax.dynamic_index_in_dim(degrees, camera, 0, keepdims=False)
        target = (camera + offset) % cameras
        slots = jnp.arange(neighbours.shape[1], dtype=jnp.int32)
        hit = jnp.logical_and(listed == target, slots < count)
        blocks.append(
            (
                split_heads(key_far),
                split_heads(value_far),
                jnp.where(jnp.any(hit), 1.0, 0.0).astype(jnp.float32),
                offset,
            )
        )

    def block_scores(qry, key_blk):
        return (
            jnp.einsum("sthd,suhd->shtu", qry, key_blk, preferred_element_type=jnp.float32) * scale
        )

    top = jnp.full((scenes, local_heads, rows), -jnp.inf, jnp.float32)
    total = jnp.zeros((scenes, local_heads, rows), jnp.float32)
    for key_blk, value_blk, weight, offset in blocks:
        block = block_scores(query, key_blk)
        peak = jnp.where(weight > 0, jnp.max(block, axis=3), -jnp.inf)
        new_top = jnp.maximum(top, peak)
        factor = jnp.exp(top - new_top)
        prob = jnp.exp(block - new_top[..., None]) * weight
        total = total * factor + jnp.sum(prob, axis=3)
        top = new_top
    lse = top + jnp.log(total)
    accum = jnp.zeros((scenes, rows, local_heads, HD), jnp.float32)
    for key_blk, value_blk, weight, offset in blocks:
        prob_low = (jnp.exp(block_scores(query, key_blk) - lse[..., None]) * weight).astype(
            jnp.bfloat16
        )
        accum = accum + jnp.einsum(
            "shtu,suhd->sthd", prob_low, value_blk, preferred_element_type=jnp.float32
        )
    attended = accum.astype(jnp.bfloat16)
    delta = jnp.transpose(
        jnp.sum(d_heads.astype(jnp.float32) * attended.astype(jnp.float32), axis=3), (0, 2, 1)
    )

    def backward_block(qry, d_q, lse_blk, delta_blk, key_blk, value_blk, weight):
        block = block_scores(qry, key_blk)
        prob = jnp.exp(block - lse_blk[..., None]) * weight
        d_prob = jnp.einsum("sthd,suhd->shtu", d_q, value_blk, preferred_element_type=jnp.float32)
        d_score = (prob * (d_prob - delta_blk[..., None])).astype(jnp.bfloat16)
        d_key = (
            jnp.einsum("shtu,sthd->suhd", d_score, qry, preferred_element_type=jnp.float32) * scale
        )
        d_value = jnp.einsum(
            "shtu,sthd->suhd", prob.astype(jnp.bfloat16), d_q, preferred_element_type=jnp.float32
        )
        d_query = None
        d_query = (
            jnp.einsum("shtu,suhd->sthd", d_score, key_blk, preferred_element_type=jnp.float32)
            * scale
        )
        return (d_query, d_key, d_value)

    d_query = jnp.zeros(query.shape, jnp.float32)
    d_key = jnp.zeros(query.shape, jnp.float32)
    d_value = jnp.zeros(query.shape, jnp.float32)
    for key_blk, value_blk, weight, offset in blocks:
        part_query, part_key, part_value = backward_block(
            query, d_heads, lse, delta, key_blk, value_blk, weight
        )
        d_query = d_query + part_query
        if offset == 0:
            d_key = part_key
            d_value = part_value
        else:
            back_key, back_value = shifted((part_key, part_value), "view", offset)
            d_key = d_key + back_key
            d_value = d_value + back_value
    grads = (
        jnp.stack([d_query, d_key, d_value]).reshape(3, scenes, rows, width).astype(jnp.bfloat16)
    )
    token_terms = jnp.einsum("jste,jde->std", grads, w_qkv, preferred_element_type=jnp.float32)[
        :, None
    ]
    d_tokens = lax.psum_scatter(token_terms, "head", scatter_dimension=3, tiled=True).astype(
        jnp.bfloat16
    )
    attended_flat = attended.reshape(scenes, rows, width)
    wqkv_terms = jnp.einsum(
        "std,jste->jde", tokens[:, 0], grads, preferred_element_type=jnp.float32
    )
    wo_terms = jnp.einsum(
        "ste,std->ed", attended_flat, d_out[:, 0], preferred_element_type=jnp.float32
    )
    d_wqkv, d_wo = (
        lax.psum_scatter(wqkv_terms, "view", scatter_dimension=1, tiled=True),
        lax.psum_scatter(wo_terms, "view", scatter_dimension=1, tiled=True),
    )
    return (d_tokens, d_wqkv, d_wo)


def body(tokens, queries, keys, values, w_qkv, w_out, d_out, neighbours, degrees):
    args = (tokens, queries, keys, values, w_qkv, w_out, d_out, neighbours, degrees)
    scenes, _, rows, width = queries.shape
    cameras, reach = neighbours.shape[0], neighbours.shape[1] // 2
    fits = (
        scenes == 2
        and lax.axis_size("head") == 2
        and scenes * (width // HD) == cameras == lax.axis_size("view")
        and rows == LANE
        and cameras == QUAD * QUAD
        and cameras >= 2 * reach + 2
    )
    return split_body(*args) if fits else halo_body(*args)


def solution(mesh):
    return jax.shard_map(
        body,
        mesh=mesh,
        in_specs=(
            P(None, "view", None, None),
            P(None, "view", None, "head"),
            P(None, "view", None, "head"),
            P(None, "view", None, "head"),
            P(None, None, "head"),
            P("head", None),
            P(None, "view", None, None),
            P(),
            P(),
        ),
        out_specs=(P(None, "view", None, "head"), P(None, "view", "head"), P("head", "view")),
        check_vma=False,
    )
```

```python
import functools

import jax
import jax.numpy as jnp
from jax import lax
from jax.experimental import pallas as pl
from jax.experimental.pallas import tpu as pltpu
from jax.sharding import PartitionSpec as P

HD = 64
LANE = 128
QUAD = 4
BF = jnp.bfloat16
F32 = jnp.float32
MIB = 2**20
OFF = -1e30


def mul(a, b):
    return jnp.dot(a, b, preferred_element_type=F32)


def mul_nt(a, b):
    return lax.dot_general(a, b, (((1,), (1,)), ((), ())), preferred_element_type=F32)


def call(kernel, name, outs, args, scratch=(), mib=16, us=1, after=(), scalars=0, inputs=None, sems=0):
    args, after = list(args), list(after)
    specs = [pl.BlockSpec(memory_space=pltpu.SMEM)] * scalars
    for arg in args[scalars:]:
        specs.append(pl.BlockSpec(memory_space=inputs or pltpu.VMEM))
    out_specs = [pl.BlockSpec(memory_space=pltpu.VMEM)] * len(outs)

    def run(pos_ref, *refs):
        kernel(pos_ref, *refs[: len(args)], *refs[len(args) + len(after) :])

    return lambda pos: pl.pallas_call(
        run,
        out_shape=[jax.ShapeDtypeStruct(dims, dtype) for dims, dtype in outs],
        in_specs=[pl.BlockSpec(memory_space=pltpu.SMEM)] + specs + [pl.BlockSpec(memory_space=pl.ANY)] * len(after),
        out_specs=out_specs,
        scratch_shapes=[pltpu.VMEM(dims, dtype) for dims, dtype in scratch] + [pltpu.SemaphoreType.DMA(())] * sems,
        compiler_params=pltpu.CompilerParams(vmem_limit_bytes=mib * MIB),
        cost_estimate=pl.CostEstimate(flops=int(us * 1.1e9), bytes_accessed=MIB, transcendentals=0),
        name=name,
    )(pos, *args, *after)


def pack_kernel(_, *refs):
    far, out_ref, near, sems = refs[:5], refs[5], refs[6:11], refs[11:]
    copies = [pltpu.make_async_copy(*trio) for trio in zip(far, near, sems)]
    for copy in copies:
        copy.start()
    q_ref, k_ref, v_ref, d_ref, w_ref = near
    scenes = range(q_ref.shape[0])

    def put(n, scene, arr):
        for view in range(out_ref.shape[0]):
            plane, quad = view // QUAD, view % QUAD
            if quad // 2 == scene:
                row = (2 * plane + quad % 2) * HD
                out_ref[view, n * HD : (n + 1) * HD] = arr[row : row + HD]

    copies[0].wait()
    for scene in scenes:
        put(0, scene, (q_ref[scene, 0].T * HD**-0.5).astype(BF))
    copies[1].wait()
    for scene in scenes:
        put(1, scene, k_ref[scene, 0].T)
    copies[2].wait()
    for scene in scenes:
        put(2, scene, v_ref[scene, 0].T)
    copies[3].wait()
    copies[4].wait()
    d_head = mul_nt(w_ref[...], d_ref[...].reshape(len(scenes) * LANE, -1)).astype(BF)
    for scene in scenes:
        put(3, scene, d_head[:, scene * LANE : (scene + 1) * LANE])


def fetch_kernel(pos_ref, t_ref, d_ref, both, t_out, d_out, *sems):
    copies = [
        pltpu.make_async_copy(ref.at[pos_ref[2], 0], out, sem)
        for ref, out, sem in zip((t_ref, d_ref), (t_out, d_out), sems)
    ]
    for n, (copy, out) in enumerate(zip(copies, (t_out, d_out))):
        copy.start()
    for n, (copy, out) in enumerate(zip(copies, (t_out, d_out))):
        copy.wait()
        both[n * LANE : (n + 1) * LANE] = out[...]


def gate(value, after):
    return lax.optimization_barrier((value, after))[0]


def places(refs, mine):
    if len(refs) == 1:
        return [(refs[0].at[n], n) for n in range(refs[0].shape[0])]
    return [(ref, mine ^ n) for n, ref in enumerate(refs)]


def rows_of(cam):
    return pl.ds(pl.multiple_of(cam * LANE, LANE), LANE)


def wrap(ref, cameras, reach, by_lane):
    low, high, edge = reach * LANE, (cameras + reach) * LANE, reach * LANE
    if by_lane:
        ref[:, :edge] = ref[:, high - edge : high]
        ref[:, high:] = ref[:, low : low + edge]
    else:
        ref[:edge] = ref[high - edge : high]
        ref[high:] = ref[low : low + edge]


def fold(acc, cameras, reach):
    low, high, edge = reach * LANE, (cameras + reach) * LANE, reach * LANE
    acc[high - edge : high] += acc[:edge]
    acc[low : low + edge] += acc[high:]


def attend_kernel(reach, pos_ref, near_ref, count_ref, in_ref, *refs):
    outs, (k_row, v_row, k_col, v_col, dk_acc, dv_acc, s_buf, p_buf, d_buf, att_buf, dq_buf) = refs[:4], refs[4:]
    cameras = in_ref.shape[0]
    span = 2 * reach + 2
    for cam in range(cameras):
        rows = slice((cam + reach) * LANE, (cam + reach + 1) * LANE)
        key, val = in_ref[cam, HD : 2 * HD], in_ref[cam, 2 * HD : 3 * HD]
        k_col[:, rows] = key
        v_col[:, rows] = val
        k_row[rows, :] = key.T
        v_row[rows, :] = val.T
    for ref, by_lane in ((k_col, True), (v_col, True), (k_row, False), (v_row, False)):
        wrap(ref, cameras, reach, by_lane)
    dk_acc[...] = jnp.zeros_like(dk_acc)
    dv_acc[...] = jnp.zeros_like(dv_acc)

    def step(i, carry):
        def pair(n):
            rows = slice(n * HD, (n + 1) * HD)
            return jnp.concatenate([in_ref[2 * i, rows], in_ref[2 * i + 1, rows]], axis=1)

        q_col, d_col = pair(0), pair(3)
        q_rows = q_col.T
        place = lax.broadcasted_iota(jnp.int32, (16, 2 * LANE), 0)
        second = lax.broadcasted_iota(jnp.int32, (16, 2 * LANE), 1) >= LANE
        target = lax.rem(2 * i + place + (cameras - reach), cameras)
        live = target == jnp.where(second, 2 * i + 1, 2 * i)
        for m in range(2 * reach):
            first, other = [jnp.where(m < count_ref[2 * i + t], near_ref[2 * i + t, m], -1) for t in range(2)]
            live = live | (target == jnp.where(second, other, first))
        offset = place - reach - jnp.where(second, 1, 0)
        bias = jnp.where(live & (jnp.abs(offset) <= reach), 0.0, OFF)
        window = pl.ds(pl.multiple_of(2 * i * LANE, 2 * LANE), span * LANE)
        top = None
        for j in range(span):
            score = mul(k_row[rows_of(2 * i + j), :], q_col)
            s_buf[j] = score
            peak = jnp.max(score, axis=0, keepdims=True) + bias[j : j + 1]
            top = peak if top is None else jnp.maximum(top, peak)
        total = jnp.zeros((8, 2 * LANE), F32)
        for j in range(span):
            prob = jnp.exp(s_buf[j] + (bias[j : j + 1] - top))
            total = total + jnp.sum(prob.reshape(LANE // 8, 8, 2 * LANE), axis=0)
            p_buf[j * LANE : (j + 1) * LANE] = prob.astype(BF)
        inv = 1.0 / jnp.sum(total, axis=0, keepdims=True)
        att = (mul(v_col[:, window], p_buf[...]) * inv).astype(BF)
        d_wide = d_col.astype(F32)
        d_low = (d_wide * inv).astype(BF)
        delta = jnp.sum(att.astype(F32) * d_low.astype(F32), axis=0, keepdims=True)
        dv_acc[window, :] += mul(p_buf[...], d_low.T)
        for j in range(span):
            rows = slice(j * LANE, (j + 1) * LANE)
            d_prob = mul(v_row[rows_of(2 * i + j), :], d_low)
            d_buf[rows] = (p_buf[rows].astype(F32) * (d_prob - delta)).astype(BF)
        dk_acc[window, :] += mul(d_buf[...], q_rows)
        d_query = (mul(k_col[:, window], d_buf[...]) * HD**-0.5).astype(BF)
        for t in range(2):
            att_buf[2 * i + t] = att[:, t * LANE : (t + 1) * LANE]
            dq_buf[2 * i + t] = d_query[:, t * LANE : (t + 1) * LANE]
        return carry

    lax.fori_loop(0, cameras // 2, step, 0)
    fold(dk_acc, cameras, reach)
    fold(dv_acc, cameras, reach)
    for ref, quad in places(outs, pos_ref[1]):
        for plane in range(cameras // QUAD):
            cam = plane * QUAD + quad
            rows = rows_of(cam + reach)
            ref[plane, :HD] = att_buf[cam]
            ref[plane, HD : 2 * HD] = dv_acc[rows, :].T.astype(BF)
            ref[plane, 2 * HD : 3 * HD] = dq_buf[cam]
            ref[plane, 3 * HD :] = dk_acc[rows, :].T.astype(BF)


def weights_kernel(planes, pos_ref, *refs):
    blocks, (tok_ref, d_ref), far, outs = refs[:4], refs[4:6], refs[6:16], refs[16:-5]
    left, left_o, tok, d_o, wide = refs[-5:]
    plane, core = pos_ref[0], pos_ref[2]
    for ref, quad in places(blocks, pos_ref[1]):
        scene, half = quad // 2, quad % 2
        for k in range(planes):
            at = rows_of(2 * k + (scene ^ core))
            block = ref.at[plane ^ k]
            left_o[pl.ds(pl.multiple_of(half * HD, HD), HD), at] = block[:HD]
            for n in range(3):
                row = pl.multiple_of((2 * n + half) * HD, HD)
                left[pl.ds(row, HD), at] = block[(n + 1) * HD : (n + 2) * HD]
    for n in range(2):
        at = slice(n * LANE, (n + 1) * LANE)
        tok[at] = tok_ref[core ^ n, 0]
        d_o[at] = d_ref[core ^ n, 0]
    for n, ref in enumerate(far[:2], 2):
        at = slice(n * LANE, (n + 1) * LANE)
        tok[at] = ref[:LANE]
        d_o[at] = ref[LANE:]
    for n, ref in enumerate(far[2:]):
        at = slice((n % 4 + 4) * LANE, (n % 4 + 5) * LANE)
        (d_o if n // 4 else tok)[at] = ref[...]
    wide[:, : 6 * HD] = mul(left[...], tok[...]).astype(BF).T
    wide[:, 6 * HD :] = mul(left_o[...], d_o[...]).astype(BF).T
    part = wide.shape[0] // (QUAD * planes)
    for ref, quad in places(outs, pos_ref[1]):
        for p in range(planes):
            rows = pl.ds(pl.multiple_of((p * QUAD + quad) * part, part), part)
            ref[p * part : (p + 1) * part] = wide[rows, :]


def sum_kernel(planes, pos_ref, *refs):
    terms, outs = refs[:QUAD], refs[QUAD:]
    part = terms[0].shape[0] // planes
    for ref, plane in places(outs, pos_ref[0]):
        rows = pl.ds(pl.multiple_of(plane * part, part), part)
        acc = terms[0][rows, :].astype(F32)
        for term in terms[1:]:
            acc = acc + term[rows, :].astype(F32)
        ref[...] = acc.astype(BF)


def finish_kernel(planes, pos_ref, *refs):
    terms, (w_ref, o_ref) = refs[:planes], refs[planes:]
    two = 2 * HD
    for ref, plane in places(terms, pos_ref[0]):
        cols = pl.ds(pl.multiple_of(plane * two, two), two)
        o_ref[:, cols] = ref[:, 3 * two :].astype(F32)
        for place, j in enumerate((2, 0, 1)):
            w_ref[j, :, cols] = ref[:, place * two : (place + 1) * two].astype(F32)


def turn_kernel(planes, pos_ref, *refs):
    blocks, outs = refs[:4], refs[4:]
    for ref, quad in places(blocks, pos_ref[1]):
        for n in range(planes):
            if len(outs) == 1:
                outs[0][n, quad] = ref[n, HD:]
            elif n:
                outs[n - 1][quad] = ref[pos_ref[0] ^ n, HD:]


def inputs_kernel(planes, pos_ref, *refs):
    blocks, far, (w_ref, mine, theirs, turned) = refs[:4], refs[4:7], refs[7:]
    plane, core = pos_ref[0], pos_ref[2]

    def put(block, home, quad):
        row = pl.ds(pl.multiple_of((2 * home + quad % 2) * HD, HD), HD)
        for place, n in enumerate((2, 0, 1)):
            turned[quad // 2, n, row] = block[place * HD : (place + 1) * HD]

    if len(far) == 1:
        for home in range(planes):
            for quad in range(QUAD):
                put(far[0][home, quad], home, quad)
    else:
        for ref, quad in places(blocks, pos_ref[1]):
            put(ref[plane, HD:], plane, quad)
        for k, ref in enumerate(far, 1):
            for quad in range(QUAD):
                put(ref[quad], plane ^ k, quad)
    left = [jnp.concatenate([turned[scene, j].T for scene in range(2)], axis=0) for j in range(3)]
    half = w_ref.shape[1] // 2
    for ref, who in ((theirs, 1 - core), (mine, core)):
        rows = pl.ds(pl.multiple_of(who * half, half), half)
        acc = mul_nt(left[0], w_ref[0, rows, :])
        for j in range(1, 3):
            acc = acc + mul_nt(left[j], w_ref[j, rows, :])
        ref[...] = acc


def split_body(tokens, queries, keys, values, w_qkv, w_out, d_out, neighbours, degrees):
    cameras = neighbours.shape[0]
    reach = neighbours.shape[1] // 2
    planes = cameras // QUAD
    scenes, _, rows, width = queries.shape
    model = tokens.shape[3]
    part = model // cameras
    view, core = lax.axis_index("view"), lax.axis_index("head")
    pos = jnp.stack([view // QUAD, view % QUAD, core]).astype(jnp.int32)
    span = 2 * reach + 2
    ext = (cameras + 2 * reach) * rows

    def along(value, pairs):
        return lax.ppermute(value, "view", pairs)

    def over_plane(values):
        if len(values) == 1:
            groups = [[p * QUAD + j for j in range(QUAD)] for p in range(planes)]
            return [lax.all_to_all(values[0], "view", 0, 0, axis_index_groups=groups, tiled=True)]
        return [values[0]] + [along(values[j], [(i, i ^ j) for i in range(cameras)]) for j in range(1, QUAD)]

    def over_column(values, first=0):
        if len(values) == 1 and values[0].shape[0] == planes:
            groups = [[p * QUAD + j for p in range(planes)] for j in range(QUAD)]
            return [lax.all_to_all(values[0], "view", 0, 0, axis_index_groups=groups, tiled=True)]
        return [
            value if k == 0 else along(value, [(i, i ^ (k * QUAD)) for i in range(cameras)])
            for k, value in enumerate(values, first)
        ]

    def other_core(value):
        return lax.ppermute(value, "head", [(0, 1), (1, 0)])

    arrays = (queries, keys, values, d_out, w_out)
    packed = call(
        pack_kernel, "pack", [((cameras, 4 * HD, rows), BF)], arrays, [(arr.shape, BF) for arr in arrays],
        56, inputs=pl.ANY, sems=len(arrays),
    )(jnp.zeros(1, jnp.int32))[0]
    packed = lax.all_to_all(packed, "view", 0, 0, tiled=True)

    own = call(fetch_kernel, "fetch", [((2 * rows, model), BF), ((rows, model), BF), ((rows, model), BF)], (tokens, d_out), (), 40, inputs=pl.ANY, sems=2)(pos)
    near = over_column([own[0]], 1)[0]
    column = [near, other_core(near)]

    blocks = call(
        functools.partial(attend_kernel, reach), "attend", [((planes, 4 * HD, rows), BF)] * QUAD, (neighbours, degrees, packed),
        [
            ((ext, HD), BF), ((ext, HD), BF), ((HD, ext), BF), ((HD, ext), BF), ((ext, HD), F32), ((ext, HD), F32),
            ((span, rows, 2 * rows), F32), ((span * rows, 2 * rows), BF), ((span * rows, 2 * rows), BF),
            ((cameras, HD, rows), BF), ((cameras, HD, rows), BF),
        ],
        32, 5, scalars=2, after=[],
    )(pos)
    done = blocks[0]
    blocks = over_plane(blocks)
    first = over_column([gate(own[1], packed)], 2)[0]
    second = over_column([gate(own[2], packed)], 2)[0]
    for far in (first, second):
        column += [far, other_core(far)]
        far = over_column([gate(far, done)], 1)[0]
        column += [far, other_core(far)]

    depth = 2 * planes * rows
    terms = call(
        functools.partial(weights_kernel, planes), "weights", [((model // QUAD, 8 * HD), BF)] * QUAD, blocks + [tokens, d_out] + column,
        [((6 * HD, depth), BF), ((2 * HD, depth), BF), ((depth, model), BF), ((depth, model), BF), ((model, 8 * HD), BF)],
        32, 3,
    )(pos)
    started = terms[:1]
    terms = call(
        functools.partial(sum_kernel, planes), "plane_sum", [((part, 8 * HD), BF)] * planes, over_plane(terms),
    )(pos)
    d_wqkv, d_wo = call(
        functools.partial(finish_kernel, planes), "finish", [((3, part, width), F32), ((part, width), F32)],
        over_column(terms),
    )(pos)

    grads = call(functools.partial(turn_kernel, planes), "turn", [((QUAD, 3 * HD, rows), BF)] * (planes - 1), blocks, after=())(pos)
    args = blocks + over_column(grads, 1) + [w_qkv]
    mine, theirs = call(
        functools.partial(inputs_kernel, planes), "inputs", [((scenes * rows, model // 2), F32)] * 2, args,
        [((scenes, 3, width, rows), BF)], 32, 2, after=started,
    )(pos)
    d_tokens = (mine + other_core(theirs)).astype(BF).reshape(scenes, 1, rows, model // 2)
    return (d_tokens, d_wqkv, d_wo.T)


def shifted(value, axis, steps):
    count = lax.axis_size(axis)
    pairs = [(source, (source + steps) % count) for source in range(count)]
    return lax.ppermute(value, axis, pairs)


def halo_body(tokens, queries, keys, values, w_qkv, w_out, d_out, neighbours, degrees):
    cameras = neighbours.shape[0]
    reach = neighbours.shape[1] // 2
    offsets = [step for step in range(-reach, reach + 1) if step != 0]
    camera = lax.axis_index("view")
    scenes, _, rows, width = queries.shape
    local_heads = width // HD
    scale = HD ** (-0.5)

    def split_heads(arr):
        return arr.reshape(scenes, rows, local_heads, HD)

    query = split_heads(queries)
    key_own = split_heads(keys)
    value_own = split_heads(values)
    d_flat = jnp.einsum(
        "std,ed->ste", d_out[:, 0], w_out, preferred_element_type=jnp.float32
    ).astype(jnp.bfloat16)
    d_heads = split_heads(d_flat)
    blocks = [(key_own, value_own, jnp.float32(1.0), 0)]
    for offset in offsets:
        key_far, value_far = shifted((keys, values), "view", -offset)
        listed = lax.dynamic_index_in_dim(neighbours, camera, 0, keepdims=False)
        count = lax.dynamic_index_in_dim(degrees, camera, 0, keepdims=False)
        target = (camera + offset) % cameras
        slots = jnp.arange(neighbours.shape[1], dtype=jnp.int32)
        hit = jnp.logical_and(listed == target, slots < count)
        blocks.append(
            (
                split_heads(key_far),
                split_heads(value_far),
                jnp.where(jnp.any(hit), 1.0, 0.0).astype(jnp.float32),
                offset,
            )
        )

    def block_scores(qry, key_blk):
        return (
            jnp.einsum("sthd,suhd->shtu", qry, key_blk, preferred_element_type=jnp.float32) * scale
        )

    top = jnp.full((scenes, local_heads, rows), -jnp.inf, jnp.float32)
    total = jnp.zeros((scenes, local_heads, rows), jnp.float32)
    for key_blk, value_blk, weight, offset in blocks:
        block = block_scores(query, key_blk)
        peak = jnp.where(weight > 0, jnp.max(block, axis=3), -jnp.inf)
        new_top = jnp.maximum(top, peak)
        factor = jnp.exp(top - new_top)
        prob = jnp.exp(block - new_top[..., None]) * weight
        total = total * factor + jnp.sum(prob, axis=3)
        top = new_top
    lse = top + jnp.log(total)
    accum = jnp.zeros((scenes, rows, local_heads, HD), jnp.float32)
    for key_blk, value_blk, weight, offset in blocks:
        prob_low = (jnp.exp(block_scores(query, key_blk) - lse[..., None]) * weight).astype(
            jnp.bfloat16
        )
        accum = accum + jnp.einsum(
            "shtu,suhd->sthd", prob_low, value_blk, preferred_element_type=jnp.float32
        )
    attended = accum.astype(jnp.bfloat16)
    delta = jnp.transpose(
        jnp.sum(d_heads.astype(jnp.float32) * attended.astype(jnp.float32), axis=3), (0, 2, 1)
    )

    def backward_block(qry, d_q, lse_blk, delta_blk, key_blk, value_blk, weight):
        block = block_scores(qry, key_blk)
        prob = jnp.exp(block - lse_blk[..., None]) * weight
        d_prob = jnp.einsum("sthd,suhd->shtu", d_q, value_blk, preferred_element_type=jnp.float32)
        d_score = (prob * (d_prob - delta_blk[..., None])).astype(jnp.bfloat16)
        d_key = (
            jnp.einsum("shtu,sthd->suhd", d_score, qry, preferred_element_type=jnp.float32) * scale
        )
        d_value = jnp.einsum(
            "shtu,sthd->suhd", prob.astype(jnp.bfloat16), d_q, preferred_element_type=jnp.float32
        )
        d_query = None
        d_query = (
            jnp.einsum("shtu,suhd->sthd", d_score, key_blk, preferred_element_type=jnp.float32)
            * scale
        )
        return (d_query, d_key, d_value)

    d_query = jnp.zeros(query.shape, jnp.float32)
    d_key = jnp.zeros(query.shape, jnp.float32)
    d_value = jnp.zeros(query.shape, jnp.float32)
    for key_blk, value_blk, weight, offset in blocks:
        part_query, part_key, part_value = backward_block(
            query, d_heads, lse, delta, key_blk, value_blk, weight
        )
        d_query = d_query + part_query
        if offset == 0:
            d_key = part_key
            d_value = part_value
        else:
            back_key, back_value = shifted((part_key, part_value), "view", offset)
            d_key = d_key + back_key
            d_value = d_value + back_value
    grads = (
        jnp.stack([d_query, d_key, d_value]).reshape(3, scenes, rows, width).astype(jnp.bfloat16)
    )
    token_terms = jnp.einsum("jste,jde->std", grads, w_qkv, preferred_element_type=jnp.float32)[
        :, None
    ]
    d_tokens = lax.psum_scatter(token_terms, "head", scatter_dimension=3, tiled=True).astype(
        jnp.bfloat16
    )
    attended_flat = attended.reshape(scenes, rows, width)
    wqkv_terms = jnp.einsum(
        "std,jste->jde", tokens[:, 0], grads, preferred_element_type=jnp.float32
    )
    wo_terms = jnp.einsum(
        "ste,std->ed", attended_flat, d_out[:, 0], preferred_element_type=jnp.float32
    )
    d_wqkv, d_wo = (
        lax.psum_scatter(wqkv_terms, "view", scatter_dimension=1, tiled=True),
        lax.psum_scatter(wo_terms, "view", scatter_dimension=1, tiled=True),
    )
    return (d_tokens, d_wqkv, d_wo)


def body(tokens, queries, keys, values, w_qkv, w_out, d_out, neighbours, degrees):
    args = (tokens, queries, keys, values, w_qkv, w_out, d_out, neighbours, degrees)
    scenes, _, rows, width = queries.shape
    cameras, reach = neighbours.shape[0], neighbours.shape[1] // 2
    fits = (
        scenes == 2
        and lax.axis_size("head") == 2
        and scenes * (width // HD) == cameras == lax.axis_size("view")
        and rows == LANE
        and cameras == QUAD * QUAD
        and cameras >= 2 * reach + 2
    )
    return split_body(*args) if fits else halo_body(*args)


def solution(mesh):
    return jax.shard_map(
        body,
        mesh=mesh,
        in_specs=(
            P(None, "view", None, None),
            P(None, "view", None, "head"),
            P(None, "view", None, "head"),
            P(None, "view", None, "head"),
            P(None, None, "head"),
            P("head", None),
            P(None, "view", None, None),
            P(),
            P(),
        ),
        out_specs=(P(None, "view", None, "head"), P(None, "view", "head"), P("head", "view")),
        check_vma=False,
    )
```

```python
import functools

import jax
import jax.numpy as jnp
from jax import lax
from jax.experimental import pallas as pl
from jax.experimental.pallas import tpu as pltpu
from jax.sharding import PartitionSpec as P

HD = 64
LANE = 128
QUAD = 4
BF = jnp.bfloat16
F32 = jnp.float32
MIB = 2**20
OFF = -1e30


def mul(a, b):
    return jnp.dot(a, b, preferred_element_type=F32)


def mul_nt(a, b):
    return lax.dot_general(a, b, (((1,), (1,)), ((), ())), preferred_element_type=F32)


def call(kernel, name, outs, args, scratch=(), mib=16, us=1, after=(), scalars=0, inputs=None, sems=0):
    args, after = list(args), list(after)
    specs = [pl.BlockSpec(memory_space=pltpu.SMEM)] * scalars
    for arg in args[scalars:]:
        specs.append(pl.BlockSpec(memory_space=inputs or pltpu.VMEM))
    out_specs = [pl.BlockSpec(memory_space=pltpu.VMEM)] * len(outs)

    def run(pos_ref, *refs):
        kernel(pos_ref, *refs[: len(args)], *refs[len(args) + len(after) :])

    return lambda pos: pl.pallas_call(
        run,
        out_shape=[jax.ShapeDtypeStruct(dims, dtype) for dims, dtype in outs],
        in_specs=[pl.BlockSpec(memory_space=pltpu.SMEM)] + specs + [pl.BlockSpec(memory_space=pl.ANY)] * len(after),
        out_specs=out_specs,
        scratch_shapes=[pltpu.VMEM(dims, dtype) for dims, dtype in scratch] + [pltpu.SemaphoreType.DMA(())] * sems,
        compiler_params=pltpu.CompilerParams(vmem_limit_bytes=mib * MIB),
        cost_estimate=pl.CostEstimate(flops=int({'attend': 0.2, 'weights': 8, 'early': 1, 'turn': 8, 'inputs': 8, 'plane_sum': 8, 'finish': 1, 'pack': 3, 'fetch': 8}.get(name, us) * 1.1e9), bytes_accessed=MIB, transcendentals=0),
        name=name,
    )(pos, *args, *after)


def pack_kernel(_, *refs):
    far, out_ref, near, sems = refs[:5], refs[5], refs[6:11], refs[11:]
    copies = [pltpu.make_async_copy(*trio) for trio in zip(far, near, sems)]
    for copy in copies:
        copy.start()
    q_ref, k_ref, v_ref, d_ref, w_ref = near
    scenes = range(q_ref.shape[0])

    def put(n, scene, arr):
        for view in range(out_ref.shape[0]):
            plane, quad = view // QUAD, view % QUAD
            if quad // 2 == scene:
                row = (2 * plane + quad % 2) * HD
                out_ref[view, n * HD : (n + 1) * HD] = arr[row : row + HD]

    copies[0].wait()
    for scene in scenes:
        put(0, scene, (q_ref[scene, 0].T * HD**-0.5).astype(BF))
    copies[1].wait()
    for scene in scenes:
        put(1, scene, k_ref[scene, 0].T)
    copies[2].wait()
    for scene in scenes:
        put(2, scene, v_ref[scene, 0].T)
    copies[3].wait()
    copies[4].wait()
    d_head = mul_nt(w_ref[...], d_ref[...].reshape(len(scenes) * LANE, -1)).astype(BF)
    for scene in scenes:
        put(3, scene, d_head[:, scene * LANE : (scene + 1) * LANE])


def fetch_kernel(pos_ref, t_ref, d_ref, both, t_out, d_out, *sems):
    copies = [
        pltpu.make_async_copy(ref.at[pos_ref[2], 0], out, sem)
        for ref, out, sem in zip((t_ref, d_ref), (t_out, d_out), sems)
    ]
    for n, (copy, out) in enumerate(zip(copies, (t_out, d_out))):
        copy.start()
    for n, (copy, out) in enumerate(zip(copies, (t_out, d_out))):
        copy.wait()
        both[n * LANE : (n + 1) * LANE] = out[...]


def gate(value, *after):
    return lax.optimization_barrier((value, *after))[0]


def places(refs, mine):
    if len(refs) == 1:
        return [(refs[0].at[n], n) for n in range(refs[0].shape[0])]
    return [(ref, mine ^ n) for n, ref in enumerate(refs)]


def rows_of(cam):
    return pl.ds(pl.multiple_of(cam * LANE, LANE), LANE)


def wrap(ref, cameras, reach, by_lane):
    low, high, edge = reach * LANE, (cameras + reach) * LANE, reach * LANE
    if by_lane:
        ref[:, :edge] = ref[:, high - edge : high]
        ref[:, high:] = ref[:, low : low + edge]
    else:
        ref[:edge] = ref[high - edge : high]
        ref[high:] = ref[low : low + edge]


def fold(acc, cameras, reach):
    low, high, edge = reach * LANE, (cameras + reach) * LANE, reach * LANE
    acc[high - edge : high] += acc[:edge]
    acc[low : low + edge] += acc[high:]


def attend_kernel(reach, pos_ref, near_ref, count_ref, in_ref, *refs):
    outs, (k_row, v_row, k_col, v_col, dk_acc, dv_acc, s_buf, p_buf, d_buf, att_buf, dq_buf) = refs[:4], refs[4:]
    cameras = in_ref.shape[0]
    span = 2 * reach + 2
    for cam in range(cameras):
        rows = slice((cam + reach) * LANE, (cam + reach + 1) * LANE)
        key, val = in_ref[cam, HD : 2 * HD], in_ref[cam, 2 * HD : 3 * HD]
        k_col[:, rows] = key
        v_col[:, rows] = val
        k_row[rows, :] = key.T
        v_row[rows, :] = val.T
    for ref, by_lane in ((k_col, True), (v_col, True), (k_row, False), (v_row, False)):
        wrap(ref, cameras, reach, by_lane)
    dk_acc[...] = jnp.zeros_like(dk_acc)
    dv_acc[...] = jnp.zeros_like(dv_acc)

    def step(i, carry):
        def pair(n):
            rows = slice(n * HD, (n + 1) * HD)
            return jnp.concatenate([in_ref[2 * i, rows], in_ref[2 * i + 1, rows]], axis=1)

        q_col, d_col = pair(0), pair(3)
        q_rows = q_col.T
        place = lax.broadcasted_iota(jnp.int32, (16, 2 * LANE), 0)
        second = lax.broadcasted_iota(jnp.int32, (16, 2 * LANE), 1) >= LANE
        target = lax.rem(2 * i + place + (cameras - reach), cameras)
        live = target == jnp.where(second, 2 * i + 1, 2 * i)
        for m in range(2 * reach):
            first, other = [jnp.where(m < count_ref[2 * i + t], near_ref[2 * i + t, m], -1) for t in range(2)]
            live = live | (target == jnp.where(second, other, first))
        offset = place - reach - jnp.where(second, 1, 0)
        bias = jnp.where(live & (jnp.abs(offset) <= reach), 0.0, OFF)
        window = pl.ds(pl.multiple_of(2 * i * LANE, 2 * LANE), span * LANE)
        top = None
        for j in range(span):
            score = mul(k_row[rows_of(2 * i + j), :], q_col)
            s_buf[j] = score
            peak = jnp.max(score, axis=0, keepdims=True) + bias[j : j + 1]
            top = peak if top is None else jnp.maximum(top, peak)
        total = jnp.zeros((8, 2 * LANE), F32)
        for j in range(span):
            prob = jnp.exp(s_buf[j] + (bias[j : j + 1] - top))
            total = total + jnp.sum(prob.reshape(LANE // 8, 8, 2 * LANE), axis=0)
            p_buf[j * LANE : (j + 1) * LANE] = prob.astype(BF)
        inv = 1.0 / jnp.sum(total, axis=0, keepdims=True)
        att = (mul(v_col[:, window], p_buf[...]) * inv).astype(BF)
        d_wide = d_col.astype(F32)
        d_low = (d_wide * inv).astype(BF)
        delta = jnp.sum(att.astype(F32) * d_low.astype(F32), axis=0, keepdims=True)
        dv_acc[window, :] += mul(p_buf[...], d_low.T)
        for j in range(span):
            rows = slice(j * LANE, (j + 1) * LANE)
            d_prob = mul(v_row[rows_of(2 * i + j), :], d_low)
            d_buf[rows] = (p_buf[rows].astype(F32) * (d_prob - delta)).astype(BF)
        dk_acc[window, :] += mul(d_buf[...], q_rows)
        d_query = (mul(k_col[:, window], d_buf[...]) * HD**-0.5).astype(BF)
        for t in range(2):
            att_buf[2 * i + t] = att[:, t * LANE : (t + 1) * LANE]
            dq_buf[2 * i + t] = d_query[:, t * LANE : (t + 1) * LANE]
        return carry

    lax.fori_loop(0, cameras // 2, step, 0)
    fold(dk_acc, cameras, reach)
    fold(dv_acc, cameras, reach)
    for ref, quad in places(outs, pos_ref[1]):
        for plane in range(cameras // QUAD):
            cam = plane * QUAD + quad
            rows = rows_of(cam + reach)
            ref[plane, :HD] = att_buf[cam]
            ref[plane, HD : 2 * HD] = dv_acc[rows, :].T.astype(BF)
            ref[plane, 2 * HD : 3 * HD] = dq_buf[cam]
            ref[plane, 3 * HD :] = dk_acc[rows, :].T.astype(BF)


def weights_kernel(planes, pos_ref, *refs):
    blocks, (tok_ref, d_ref), far, outs = refs[:4], refs[4:6], refs[6:16], refs[16:-5]
    left, left_o, tok, d_o, wide = refs[-5:]
    plane, core = pos_ref[0], pos_ref[2]
    for ref, quad in places(blocks, pos_ref[1]):
        scene, half = quad // 2, quad % 2
        for k in range(planes):
            at = rows_of(2 * k + (scene ^ core))
            block = ref.at[plane ^ k]
            left_o[pl.ds(pl.multiple_of(half * HD, HD), HD), at] = block[:HD]
            for n in range(3):
                row = pl.multiple_of((2 * n + half) * HD, HD)
                left[pl.ds(row, HD), at] = block[(n + 1) * HD : (n + 2) * HD]
    for n in range(2):
        at = slice(n * LANE, (n + 1) * LANE)
        tok[at] = tok_ref[core ^ n, 0]
        d_o[at] = d_ref[core ^ n, 0]
    for n, ref in enumerate(far[:2], 2):
        at = slice(n * LANE, (n + 1) * LANE)
        tok[at] = ref[:LANE]
        d_o[at] = ref[LANE:]
    for n, ref in enumerate(far[2:]):
        at = slice((n % 4 + 4) * LANE, (n % 4 + 5) * LANE)
        (d_o if n // 4 else tok)[at] = ref[...]
    wide[:, : 6 * HD] = mul(left[...], tok[...]).astype(BF).T
    wide[:, 6 * HD :] = mul(left_o[...], d_o[...]).astype(BF).T
    part = wide.shape[0] // (QUAD * planes)
    for ref, quad in places(outs, pos_ref[1]):
        for p in range(planes):
            rows = pl.ds(pl.multiple_of((p * QUAD + quad) * part, part), part)
            ref[p * part : (p + 1) * part] = wide[rows, :]


def sum_kernel(planes, pos_ref, *refs):
    terms, outs = refs[:QUAD], refs[QUAD:]
    part = terms[0].shape[0] // planes
    for ref, plane in places(outs, pos_ref[0]):
        rows = pl.ds(pl.multiple_of(plane * part, part), part)
        acc = terms[0][rows, :].astype(F32)
        for term in terms[1:]:
            acc = acc + term[rows, :].astype(F32)
        ref[...] = acc.astype(BF)


def finish_kernel(planes, pos_ref, *refs):
    terms, (w_ref, o_ref) = refs[:planes], refs[planes:]
    two = 2 * HD
    for ref, plane in places(terms, pos_ref[0]):
        cols = pl.ds(pl.multiple_of(plane * two, two), two)
        o_ref[:, cols] = ref[:, 3 * two :].astype(F32)
        for place, j in enumerate((2, 0, 1)):
            w_ref[j, :, cols] = ref[:, place * two : (place + 1) * two].astype(F32)


def turn_kernel(planes, pos_ref, *refs):
    blocks, outs = refs[:4], refs[4:]
    for ref, quad in places(blocks, pos_ref[1]):
        for n in range(planes):
            if len(outs) == 1:
                outs[0][n, quad] = ref[n, HD:]
            elif n:
                outs[n - 1][quad] = ref[pos_ref[0] ^ n, HD:]


def inputs_kernel(planes, pos_ref, *refs):
    blocks, far, (w_ref, mine, theirs, turned) = refs[:4], refs[4:7], refs[7:]
    plane, core = pos_ref[0], pos_ref[2]

    def put(block, home, quad):
        row = pl.ds(pl.multiple_of((2 * home + quad % 2) * HD, HD), HD)
        for place, n in enumerate((2, 0, 1)):
            turned[quad // 2, n, row] = block[place * HD : (place + 1) * HD]

    if len(far) == 1:
        for home in range(planes):
            for quad in range(QUAD):
                put(far[0][home, quad], home, quad)
    else:
        for ref, quad in places(blocks, pos_ref[1]):
            put(ref[plane, HD:], plane, quad)
        for k, ref in enumerate(far, 1):
            for quad in range(QUAD):
                put(ref[quad], plane ^ k, quad)
    left = [jnp.concatenate([turned[scene, j].T for scene in range(2)], axis=0) for j in range(3)]
    half = w_ref.shape[1] // 2
    for ref, who in ((theirs, 1 - core), (mine, core)):
        rows = pl.ds(pl.multiple_of(who * half, half), half)
        acc = mul_nt(left[0], w_ref[0, rows, :])
        for j in range(1, 3):
            acc = acc + mul_nt(left[j], w_ref[j, rows, :])
        ref[...] = acc


def split_body(tokens, queries, keys, values, w_qkv, w_out, d_out, neighbours, degrees):
    cameras = neighbours.shape[0]
    reach = neighbours.shape[1] // 2
    planes = cameras // QUAD
    scenes, _, rows, width = queries.shape
    model = tokens.shape[3]
    part = model // cameras
    view, core = lax.axis_index("view"), lax.axis_index("head")
    pos = jnp.stack([view // QUAD, view % QUAD, core]).astype(jnp.int32)
    span = 2 * reach + 2
    ext = (cameras + 2 * reach) * rows

    def along(value, pairs):
        return lax.ppermute(value, "view", pairs)

    def over_plane(values):
        if len(values) == 1:
            groups = [[p * QUAD + j for j in range(QUAD)] for p in range(planes)]
            return [lax.all_to_all(values[0], "view", 0, 0, axis_index_groups=groups, tiled=True)]
        return [values[0]] + [along(values[j], [(i, i ^ j) for i in range(cameras)]) for j in range(1, QUAD)]

    def over_column(values, first=0):
        if len(values) == 1 and values[0].shape[0] == planes:
            groups = [[p * QUAD + j for p in range(planes)] for j in range(QUAD)]
            return [lax.all_to_all(values[0], "view", 0, 0, axis_index_groups=groups, tiled=True)]
        return [
            value if k == 0 else along(value, [(i, i ^ (k * QUAD)) for i in range(cameras)])
            for k, value in enumerate(values, first)
        ]

    def other_core(value):
        return lax.ppermute(value, "head", [(0, 1), (1, 0)])

    arrays = (queries, keys, values, d_out, w_out)
    packed = call(
        pack_kernel, "pack", [((cameras, 4 * HD, rows), BF)], arrays, [(arr.shape, BF) for arr in arrays],
        56, inputs=pl.ANY, sems=len(arrays),
    )(jnp.zeros(1, jnp.int32))[0]
    packed = lax.all_to_all(packed, "view", 0, 0, tiled=True)

    own = call(fetch_kernel, "fetch", [((2 * rows, model), BF), ((rows, model), BF), ((rows, model), BF)], (tokens, d_out), (), 40, inputs=pl.ANY, sems=2)(pos)
    near = over_column([own[0]], 1)[0]
    column = [near, other_core(near)]

    blocks = call(
        functools.partial(attend_kernel, reach), "attend", [((planes, 4 * HD, rows), BF)] * QUAD, (neighbours, degrees, packed),
        [
            ((ext, HD), BF), ((ext, HD), BF), ((HD, ext), BF), ((HD, ext), BF), ((ext, HD), F32), ((ext, HD), F32),
            ((span, rows, 2 * rows), F32), ((span * rows, 2 * rows), BF), ((span * rows, 2 * rows), BF),
            ((cameras, HD, rows), BF), ((cameras, HD, rows), BF),
        ],
        32, 13, scalars=2, after=[],
    )(pos)
    done = blocks[0]
    blocks = over_plane(blocks)
    first = over_column([gate(own[1], packed)], 2)[0]
    second = over_column([gate(own[2], packed)], 2)[0]
    column += [first, other_core(first)]
    first = over_column([gate(first, done)], 1)[0]
    grads = call(functools.partial(turn_kernel, planes), "turn", [((QUAD, 3 * HD, rows), BF)] * (planes - 1), blocks, after=())(pos)
    column += [first, other_core(first)]
    column += [second, other_core(second)]
    second = over_column([gate(second, done)], 1)[0]
    column += [second, other_core(second)]

    depth = 2 * planes * rows
    terms = call(
        functools.partial(weights_kernel, planes), "weights", [((model // QUAD, 8 * HD), BF)] * QUAD, blocks + [tokens, d_out] + column,
        [((6 * HD, depth), BF), ((2 * HD, depth), BF), ((depth, model), BF), ((depth, model), BF), ((model, 8 * HD), BF)],
        32, 3,
    )(pos)
    started = terms[:1]
    terms = call(
        functools.partial(sum_kernel, planes), "plane_sum", [((part, 8 * HD), BF)] * planes, over_plane(terms),
    )(pos)
    d_wqkv, d_wo = call(
        functools.partial(finish_kernel, planes), "finish", [((3, part, width), F32), ((part, width), F32)],
        over_column(terms),
    )(pos)

    args = blocks + over_column(grads, 1) + [w_qkv]
    mine, theirs = call(
        functools.partial(inputs_kernel, planes), "inputs", [((scenes * rows, model // 2), F32)] * 2, args,
        [((scenes, 3, width, rows), BF)], 32, 2,
    )(pos)
    d_tokens = (mine + other_core(theirs)).astype(BF).reshape(scenes, 1, rows, model // 2)
    return (d_tokens, d_wqkv, d_wo.T)


def shifted(value, axis, steps):
    count = lax.axis_size(axis)
    pairs = [(source, (source + steps) % count) for source in range(count)]
    return lax.ppermute(value, axis, pairs)


def halo_body(tokens, queries, keys, values, w_qkv, w_out, d_out, neighbours, degrees):
    cameras = neighbours.shape[0]
    reach = neighbours.shape[1] // 2
    offsets = [step for step in range(-reach, reach + 1) if step != 0]
    camera = lax.axis_index("view")
    scenes, _, rows, width = queries.shape
    local_heads = width // HD
    scale = HD ** (-0.5)

    def split_heads(arr):
        return arr.reshape(scenes, rows, local_heads, HD)

    query = split_heads(queries)
    key_own = split_heads(keys)
    value_own = split_heads(values)
    d_flat = jnp.einsum(
        "std,ed->ste", d_out[:, 0], w_out, preferred_element_type=jnp.float32
    ).astype(jnp.bfloat16)
    d_heads = split_heads(d_flat)
    blocks = [(key_own, value_own, jnp.float32(1.0), 0)]
    for offset in offsets:
        key_far, value_far = shifted((keys, values), "view", -offset)
        listed = lax.dynamic_index_in_dim(neighbours, camera, 0, keepdims=False)
        count = lax.dynamic_index_in_dim(degrees, camera, 0, keepdims=False)
        target = (camera + offset) % cameras
        slots = jnp.arange(neighbours.shape[1], dtype=jnp.int32)
        hit = jnp.logical_and(listed == target, slots < count)
        blocks.append(
            (
                split_heads(key_far),
                split_heads(value_far),
                jnp.where(jnp.any(hit), 1.0, 0.0).astype(jnp.float32),
                offset,
            )
        )

    def block_scores(qry, key_blk):
        return (
            jnp.einsum("sthd,suhd->shtu", qry, key_blk, preferred_element_type=jnp.float32) * scale
        )

    top = jnp.full((scenes, local_heads, rows), -jnp.inf, jnp.float32)
    total = jnp.zeros((scenes, local_heads, rows), jnp.float32)
    for key_blk, value_blk, weight, offset in blocks:
        block = block_scores(query, key_blk)
        peak = jnp.where(weight > 0, jnp.max(block, axis=3), -jnp.inf)
        new_top = jnp.maximum(top, peak)
        factor = jnp.exp(top - new_top)
        prob = jnp.exp(block - new_top[..., None]) * weight
        total = total * factor + jnp.sum(prob, axis=3)
        top = new_top
    lse = top + jnp.log(total)
    accum = jnp.zeros((scenes, rows, local_heads, HD), jnp.float32)
    for key_blk, value_blk, weight, offset in blocks:
        prob_low = (jnp.exp(block_scores(query, key_blk) - lse[..., None]) * weight).astype(
            jnp.bfloat16
        )
        accum = accum + jnp.einsum(
            "shtu,suhd->sthd", prob_low, value_blk, preferred_element_type=jnp.float32
        )
    attended = accum.astype(jnp.bfloat16)
    delta = jnp.transpose(
        jnp.sum(d_heads.astype(jnp.float32) * attended.astype(jnp.float32), axis=3), (0, 2, 1)
    )

    def backward_block(qry, d_q, lse_blk, delta_blk, key_blk, value_blk, weight):
        block = block_scores(qry, key_blk)
        prob = jnp.exp(block - lse_blk[..., None]) * weight
        d_prob = jnp.einsum("sthd,suhd->shtu", d_q, value_blk, preferred_element_type=jnp.float32)
        d_score = (prob * (d_prob - delta_blk[..., None])).astype(jnp.bfloat16)
        d_key = (
            jnp.einsum("shtu,sthd->suhd", d_score, qry, preferred_element_type=jnp.float32) * scale
        )
        d_value = jnp.einsum(
            "shtu,sthd->suhd", prob.astype(jnp.bfloat16), d_q, preferred_element_type=jnp.float32
        )
        d_query = None
        d_query = (
            jnp.einsum("shtu,suhd->sthd", d_score, key_blk, preferred_element_type=jnp.float32)
            * scale
        )
        return (d_query, d_key, d_value)

    d_query = jnp.zeros(query.shape, jnp.float32)
    d_key = jnp.zeros(query.shape, jnp.float32)
    d_value = jnp.zeros(query.shape, jnp.float32)
    for key_blk, value_blk, weight, offset in blocks:
        part_query, part_key, part_value = backward_block(
            query, d_heads, lse, delta, key_blk, value_blk, weight
        )
        d_query = d_query + part_query
        if offset == 0:
            d_key = part_key
            d_value = part_value
        else:
            back_key, back_value = shifted((part_key, part_value), "view", offset)
            d_key = d_key + back_key
            d_value = d_value + back_value
    grads = (
        jnp.stack([d_query, d_key, d_value]).reshape(3, scenes, rows, width).astype(jnp.bfloat16)
    )
    token_terms = jnp.einsum("jste,jde->std", grads, w_qkv, preferred_element_type=jnp.float32)[
        :, None
    ]
    d_tokens = lax.psum_scatter(token_terms, "head", scatter_dimension=3, tiled=True).astype(
        jnp.bfloat16
    )
    attended_flat = attended.reshape(scenes, rows, width)
    wqkv_terms = jnp.einsum(
        "std,jste->jde", tokens[:, 0], grads, preferred_element_type=jnp.float32
    )
    wo_terms = jnp.einsum(
        "ste,std->ed", attended_flat, d_out[:, 0], preferred_element_type=jnp.float32
    )
    d_wqkv, d_wo = (
        lax.psum_scatter(wqkv_terms, "view", scatter_dimension=1, tiled=True),
        lax.psum_scatter(wo_terms, "view", scatter_dimension=1, tiled=True),
    )
    return (d_tokens, d_wqkv, d_wo)


def body(tokens, queries, keys, values, w_qkv, w_out, d_out, neighbours, degrees):
    args = (tokens, queries, keys, values, w_qkv, w_out, d_out, neighbours, degrees)
    scenes, _, rows, width = queries.shape
    cameras, reach = neighbours.shape[0], neighbours.shape[1] // 2
    fits = (
        scenes == 2
        and lax.axis_size("head") == 2
        and scenes * (width // HD) == cameras == lax.axis_size("view")
        and rows == LANE
        and cameras == QUAD * QUAD
        and cameras >= 2 * reach + 2
    )
    return split_body(*args) if fits else halo_body(*args)


def solution(mesh):
    return jax.shard_map(
        body,
        mesh=mesh,
        in_specs=(
            P(None, "view", None, None),
            P(None, "view", None, "head"),
            P(None, "view", None, "head"),
            P(None, "view", None, "head"),
            P(None, None, "head"),
            P("head", None),
            P(None, "view", None, None),
            P(),
            P(),
        ),
        out_specs=(P(None, "view", None, "head"), P(None, "view", "head"), P("head", "view")),
        check_vma=False,
    )
```
